32 devices in a mesh: rows: 8 (over z, x), heads: 4 (over y, core).
Axes of the slice: x: 2, y: 2, z: 4, core: 2. Of those that a mesh axis runs over, the one named last changes fastest.
Arguments:
- pair_rep: bfloat16 [12, 256, 256, 128], P(None, 'rows'), may hold values from -6 to 6
- lengths: int32 [12], replicated, may hold values from 64 to 256, as said below
- proj_weight: float32 [128, 512], P('rows', 'heads'), may hold values from -0.5 to 0.5
- bias_weight: float32 [128, 4], P('rows', 'heads'), may hold values from -0.5 to 0.5
- out_weight: float32 [128, 128], P('heads', 'rows'), may hold values from -3 to 3
- up_weight: float32 [128, 512], P(('rows', 'heads')), may hold values from -0.5 to 0.5
- down_weight: float32 [512, 128], P(('rows', 'heads')), may hold values from -0.25 to 0.25
- norm_gains: float32 [4, 128], P(None, ('rows', 'heads')), may hold values from -1 to 1.4, as said below
- proj_moment: float32 [128, 512], P('rows', 'heads'), may hold values from -256 to 256
- bias_moment: float32 [128, 4], P('rows', 'heads'), may hold values from -512 to 512
- out_moment: float32 [128, 128], P('heads', 'rows'), may hold values from -256 to 256
- up_moment: float32 [128, 512], P(('rows', 'heads')), may hold values from -2560 to 2560
- down_moment: float32 [512, 128], P(('rows', 'heads')), may hold values from -2560 to 2560
- gains_moment: float32 [4, 128], P(None, ('rows', 'heads')), may hold values from -5120 to 5120
- proj_average: float32 [128, 512], P('rows', 'heads'), may hold values from -0.5 to 0.5
- bias_average: float32 [128, 4], P('rows', 'heads'), may hold values from -0.5 to 0.5
- out_average: float32 [128, 128], P('heads', 'rows'), may hold values from -3 to 3
- up_average: float32 [128, 512], P(('rows', 'heads')), may hold values from -0.5 to 0.5
- down_average: float32 [512, 128], P(('rows', 'heads')), may hold values from -0.25 to 0.25
- gains_average: float32 [4, 128], P(None, ('rows', 'heads')), may hold values from 0.5 to 1.5
- cotangent: bfloat16 [12, 256, 256, 128], P(None, 'rows', 'heads'), may hold values from -6 to 6
Outputs:
- result: bfloat16 [12, 256, 256, 128], P(None, 'rows', 'heads')
- d_pair: bfloat16 [12, 256, 256, 128], P(None, 'rows', 'heads')
- new_proj: float32 [128, 512], P('rows', 'heads')
- new_bias: float32 [128, 4], P('rows', 'heads')
- new_out: float32 [128, 128], P('heads', 'rows')
- new_up: float32 [128, 512], P(('rows', 'heads'))
- new_down: float32 [512, 128], P(('rows', 'heads'))
- new_gains: float32 [4, 128], P(None, ('rows', 'heads'))
- proj_moment_new: float32 [128, 512], P('rows', 'heads')
- bias_moment_new: float32 [128, 4], P('rows', 'heads')
- out_moment_new: float32 [128, 128], P('heads', 'rows')
- up_moment_new: float32 [128, 512], P(('rows', 'heads'))
- down_moment_new: float32 [512, 128], P(('rows', 'heads'))
- gains_moment_new: float32 [4, 128], P(None, ('rows', 'heads'))
- proj_average_new: float32 [128, 512], P('rows', 'heads')
- bias_average_new: float32 [128, 4], P('rows', 'heads')
- out_average_new: float32 [128, 128], P('heads', 'rows')
- up_average_new: float32 [128, 512], P(('rows', 'heads'))
- down_average_new: float32 [512, 128], P(('rows', 'heads'))
- gains_average_new: float32 [4, 128], P(None, ('rows', 'heads'))
The draws below stay inside these ranges and needn't reach their ends.
Inputs may be any that keep to these rules, and one draw needn't show every extreme that they name: `lengths`: each item's residues 0 to its length - 1 are real; one item has all 256. `norm_gains`: rows 0 and 2 are gains, rows 1 and 3 shifts.
All inputs are finite; a program needn't handle non-finite values.
Results may differ from the reference program's by a relative error of at most 0.025.
Values may be sent and summed in bfloat16 or wider, within the bound.
A program may use at most 576 MiB of HBM per device.

```python
import math
import jax
import jax.numpy as jnp
from jax import lax

C = 128
H = 4
DH = 32
HID = 512
RES = 256
ITEMS = 12


def draw_lengths(key, part):
    key = jax.random.fold_in(key, 11)
    first_key, second_key = jax.random.split(key)
    drawn = jax.random.randint(first_key, (ITEMS,), RES // 4, RES + 1)
    chosen = jax.random.randint(second_key, (), 0, ITEMS)
    return jnp.where(jnp.arange(ITEMS) == chosen, RES, drawn).astype(jnp.int32)


def draw_norm_gains(key, part):
    key = jax.random.fold_in(key, 17)
    first_key, second_key = jax.random.split(key)
    gain_rows = 1.0 + 0.4 * jax.random.uniform(first_key, (4, C), jnp.float32, -1.0, 1.0)
    shift_rows = jnp.clip(0.3 * jax.random.normal(second_key, (4, C), jnp.float32), -1.0, 1.0)
    is_gain = (jnp.arange(4) % 2 == 0)[:, None]
    return jnp.where(is_gain, gain_rows, shift_rows).astype(jnp.float32)


def level_of(rng, extent, cuts, least, top_value):
    loudness = 1.0
    for position, parts in cuts:
        steps = jax.random.uniform(jax.random.fold_in(jax.random.fold_in(rng, 6), position), (parts,), jnp.float32, least / len(cuts), top_value / len(cuts))
        loudness = loudness * jnp.repeat(jnp.exp(steps), extent[position] // parts).reshape((-1,) + (1,) * (len(extent) - 1 - position))
    return loudness


def scatter_about(stream_key, dims, scale, bound, shards=(), kind=jnp.bfloat16):
    array = jax.random.normal(stream_key, dims, jnp.float32) * scale
    if len(shards) > 0:
        array = level_of(stream_key, dims, shards, -0.22, 0.18) * array
    return jnp.clip(array, min=-bound, max=bound).astype(kind)


def setup_inputs(seed: int = 0) -> dict:
    seeds = jax.random.split(jax.random.key(seed), 22)
    return {
        "pair_rep": scatter_about(seeds[0], (ITEMS, RES, RES, C), 1.0, 6.0, ((1, 8),)),
        "lengths": draw_lengths(jax.random.fold_in(seeds[21], 71), 0),
        "proj_weight": scatter_about(seeds[2], (C, H * 4 * DH), C ** -0.5, 0.5, ((0, 8), (1, 4)), jnp.float32),
        "bias_weight": scatter_about(seeds[3], (C, H), C ** -0.5, 0.5, ((0, 8), (1, 4)), jnp.float32),
        "out_weight": scatter_about(seeds[4], (H * DH, C), 4 ** -0.5, 3.0, ((0, 4), (1, 8)), jnp.float32),
        "up_weight": scatter_about(seeds[5], (C, HID), C ** -0.5, 0.5, ((0, 32),), jnp.float32),
        "down_weight": scatter_about(seeds[6], (HID, C), HID ** -0.5, 0.25, ((0, 32),), jnp.float32),
        "norm_gains": draw_norm_gains(jax.random.fold_in(seeds[21], 71), 0),
        "proj_moment": scatter_about(seeds[8], (C, H * 4 * DH), (0.05 * (ITEMS * RES * RES) ** 0.5), 256.0, ((0, 8), (1, 4)), jnp.float32),
        "bias_moment": scatter_about(seeds[9], (C, H), (0.3 * (ITEMS * RES * 32) ** 0.5), 512.0, ((0, 8), (1, 4)), jnp.float32),
        "out_moment": scatter_about(seeds[10], (H * DH, C), (0.05 * (ITEMS * RES * RES) ** 0.5), 256.0, ((0, 4), (1, 8)), jnp.float32),
        "up_moment": scatter_about(seeds[11], (C, HID), (0.5 * (ITEMS * RES * RES) ** 0.5), 2560.0, ((0, 32),), jnp.float32),
        "down_moment": scatter_about(seeds[12], (HID, C), (0.5 * (ITEMS * RES * RES) ** 0.5), 2560.0, ((0, 32),), jnp.float32),
        "gains_moment": scatter_about(seeds[13], (4, C), (1.0 * (ITEMS * RES * RES) ** 0.5), 5120.0, ((1, 32),), jnp.float32),
        "proj_average": scatter_about(seeds[14], (C, H * 4 * DH), C ** -0.5, 0.5, ((0, 8), (1, 4)), jnp.float32),
        "bias_average": scatter_about(seeds[15], (C, H), C ** -0.5, 0.5, ((0, 8), (1, 4)), jnp.float32),
        "out_average": scatter_about(seeds[16], (H * DH, C), 4 ** -0.5, 3.0, ((0, 4), (1, 8)), jnp.float32),
        "up_average": scatter_about(seeds[17], (C, HID), C ** -0.5, 0.5, ((0, 32),), jnp.float32),
        "down_average": scatter_about(seeds[18], (HID, C), HID ** -0.5, 0.25, ((0, 32),), jnp.float32),
        "gains_average": jnp.clip(1.0 + 0.1 * jax.random.normal(seeds[19], (4, C), jnp.float32), 0.5, 1.5),
        "cotangent": scatter_about(seeds[20], (ITEMS, RES, RES, C), 1.0, 6.0, ((1, 8), (2, 4))),
    }


@jax.custom_vjp
def low(v):
    return lax.optimization_barrier(v.astype(jnp.bfloat16)).astype(jnp.float32)

@jax.custom_vjp
def low_back(v):
    return v

def low_keep(v):
    return (low(v), None)

def low_pass(kept, grad):
    return (grad,)

def back_keep(v):
    return (v, None)

def back_low(kept, grad):
    return (low(grad),)
low.defvjp(low_keep, low_pass)
low_back.defvjp(back_keep, back_low)
EPSILON = 1e-05
MOMENTUM = 0.9
AVERAGE = 0.6
RATES = (0.5, 0.3, 3.0, 0.05, 0.03, 0.1)

def highest_dot(left, right):
    return jnp.dot(left, right, precision=lax.Precision.HIGHEST, preferred_element_type=jnp.float32)

def layer_norm(values, gain_row, shift_row):
    centre = lax.optimization_barrier(jnp.mean(values, axis=-1, keepdims=True))
    shifted = values - centre
    spread = lax.rsqrt(lax.optimization_barrier(jnp.mean(shifted * shifted, axis=-1, keepdims=True)) + EPSILON)
    return shifted * spread * gain_row + shift_row

def head_branch(normed, proj_block, bias_column, out_block, key_mask):
    shared = low_back(normed)
    projected = low(low_back(highest_dot(shared, proj_block)))
    bias_map = low(low_back(highest_dot(shared, bias_column)))
    query_part = projected[..., :DH]
    key_part = projected[..., DH:2 * DH]
    values = projected[..., 2 * DH:3 * DH]
    gate_in = projected[..., 3 * DH:]
    logits = jnp.einsum('ijd,ikd->ijk', query_part, key_part, precision=lax.Precision.HIGHEST) * (1.0 / math.sqrt(DH)) + bias_map[None]
    logits = jnp.where(key_mask[None, None, :], low_back(logits), -1000000000.0)
    probs_full = jax.nn.softmax(logits, axis=-1)
    blended = low_back(jnp.einsum('ijk,ikd->ijd', low(probs_full), values, precision=lax.Precision.HIGHEST))
    gated_out = low_back(low(jax.nn.sigmoid(gate_in) * blended))
    return low(highest_dot(gated_out, out_block))

def item_layer(weights, pair_item, length):
    proj_weight, bias_weight, out_weight, up_weight, down_weight, norm_gains = weights
    gain_low = low(norm_gains)
    normed = low(layer_norm(pair_item, gain_low[0], gain_low[1]))
    key_mask = jnp.arange(RES) < length
    proj_low = low(proj_weight)
    bias_low = low(bias_weight)
    out_low = low(out_weight)
    branch = jnp.zeros_like(pair_item)
    for head_index in range(H):
        branch = branch + jax.checkpoint(head_branch)(normed, proj_low[:, head_index * 4 * DH:(head_index + 1) * 4 * DH], bias_low[:, head_index], out_low[head_index * DH:(head_index + 1) * DH], key_mask)
    middle = pair_item + low_back(branch)
    shaped = low(layer_norm(middle, gain_low[2], gain_low[3]))
    hidden_pre = low_back(highest_dot(shaped, low(up_weight)))
    hidden = low(jax.nn.silu(hidden_pre))
    return middle + highest_dot(hidden, low(down_weight))

def reference(pair_rep, lengths, proj_weight, bias_weight, out_weight, up_weight, down_weight, norm_gains, proj_moment, bias_moment, out_moment, up_moment, down_moment, gains_moment, proj_average, bias_average, out_average, up_average, down_average, gains_average, cotangent):
    weights = (proj_weight, bias_weight, out_weight, up_weight, down_weight, norm_gains)
    grad_zero = jax.tree.map(jnp.zeros_like, weights)

    def item_step(grad_total, inputs):
        pair_item, length, cot_item = inputs
        layer_out, pullback = jax.vjp(lambda wts, pair_f: item_layer(wts, pair_f, length), weights, pair_item.astype(jnp.float32))
        grads, d_item = pullback(cot_item.astype(jnp.float32))
        grad_total = jax.tree.map(lambda first, second: first + second, grad_total, grads)
        return (grad_total, (layer_out.astype(jnp.bfloat16), d_item.astype(jnp.bfloat16)))
    grads, (result, d_pair) = lax.scan(item_step, grad_zero, (pair_rep, lengths, cotangent))
    root_pairs = math.sqrt(ITEMS * RES * RES)
    moments = (proj_moment, bias_moment, out_moment, up_moment, down_moment, gains_moment)
    averages = (proj_average, bias_average, out_average, up_average, down_average, gains_average)
    new_weights = []
    new_moments = []
    new_averages = []
    for weight, gradient, moment, average, step_rate in zip(weights, grads, moments, averages, RATES):
        moment_next = MOMENTUM * moment + gradient
        weight_next = weight - step_rate / root_pairs * (gradient + MOMENTUM * moment_next)
        new_weights.append(weight_next)
        new_moments.append(moment_next)
        new_averages.append(AVERAGE * average + (1.0 - AVERAGE) * weight_next)
    return (result, d_pair, new_weights[0], new_weights[1], new_weights[2], new_weights[3], new_weights[4], new_weights[5], new_moments[0], new_moments[1], new_moments[2], new_moments[3], new_moments[4], new_moments[5], new_averages[0], new_averages[1], new_averages[2], new_averages[3], new_averages[4], new_averages[5])
```

```python
import math
import functools
import jax
import jax.numpy as jnp
from jax import lax
from jax.experimental import pallas as pl
from jax.experimental.pallas import tpu as pltpu
from jax.sharding import PartitionSpec as P

EPSILON = 1e-05
LOG2E = 1.4426950408889634
LN2 = 0.6931471805599453
LOW = jnp.bfloat16
FULL = jnp.float32


def dot_nt(a, b):
    return lax.dot_general(a, b, (((1,), (1,)), ((), ())), preferred_element_type=FULL)


def dot_nn(a, b):
    return lax.dot_general(a, b, (((1,), (0,)), ((), ())), preferred_element_type=FULL)


def dot_tn(a, b):
    return lax.dot_general(a, b, (((0,), (0,)), ((), ())), preferred_element_type=FULL)


def normalize(values):
    centre = jnp.mean(values, axis=-1, keepdims=True)
    shifted = values - centre
    spread = lax.rsqrt(jnp.mean(shifted * shifted, axis=-1, keepdims=True) + EPSILON)
    return (shifted * spread, spread)


def main_kernel(
    len_ref, q_ref,
    x_ref, xq_ref, cot_ref, bias_ref,
    wkv_ref, wqg_ref, wo_ref, up_ref, down_ref, gain_ref,
    gkv_in, gqg_in, gout_in, gup_in, gdown_in, ggain_in,
    res_ref, dmid_ref, own0_ref, own1_ref, sib0_ref, sib1_ref, dbias_ref,
    gkv_ref, gqg_ref, gout_ref, gup_ref, gdown_ref, ggain_ref,
    n_s, kv_s, dkv_s, e_s, nq_s, q_s, o_s, r_s, g_s, dos_s, xn_s, hid_s, dpre_s, sh_s, dml_s, gated_s, dqg_s,
    bias_s, dbias_s, dn_s,
    *, start, ib, heads, width, variants, tb, depth, omode, qmode,
):
    item = pl.program_id(0)
    blk = pl.program_id(1)
    length = len_ref[start + item]
    q = q_ref[0]
    res = x_ref.shape[2]
    c = x_ref.shape[3]
    quarter = res // 4
    tokens = ib * quarter
    hj = heads * quarter
    score = 1.0 / math.sqrt(width)

    lane_head = lax.broadcasted_iota(jnp.int32, (1, c), 1) // width
    head_masks = [(lane_head == h).astype(FULL) for h in range(heads)]

    def block_diag(v):
        return jnp.concatenate([(v * m).astype(LOW) for m in head_masks], axis=0)

    diag_mask = (
        lax.broadcasted_iota(jnp.int32, (c, hj), 0) // width
        == lax.broadcasted_iota(jnp.int32, (c, hj), 1) // quarter
    )

    def compact(t):
        t = jnp.where(diag_mask, t, 0.0)
        t = t[:, : hj // 2] + t[:, hj // 2 :]
        t = t.T
        return t[:quarter] + t[quarter:]

    @pl.when(jnp.logical_and(item == 0, blk == 0))
    def _():
        gkv_ref[...] = gkv_in[...]
        gqg_ref[...] = gqg_in[...]
        gout_ref[...] = gout_in[...]
        gup_ref[...] = gup_in[...]
        gdown_ref[...] = gdown_in[...]
        ggain_ref[...] = ggain_in[...]

    @pl.when(blk == 0)
    def _():
        b = bias_ref[0].astype(FULL).T * LOG2E
        real = lax.broadcasted_iota(jnp.int32, (res, hj), 0) < length
        bias_s[...] = jnp.where(real, b, -1e9)
        dbias_s[...] = jnp.zeros_like(dbias_s)

    g0 = gain_ref[0:1, :]
    g1 = gain_ref[1:2, :]
    g2 = gain_ref[2:3, :]
    g3 = gain_ref[3:4, :]

    xq = xq_ref[0].reshape(tokens, c).astype(FULL)
    nq = (normalize(xq)[0] * g0 + g1).astype(LOW)
    nq_s[...] = nq
    qg = dot_nn(nq, wqg_ref[...]).astype(LOW).astype(FULL)
    q_s[...] = (qg[:, :c] * (score * LOG2E)).astype(LOW).reshape(ib, quarter, c)
    g_s[...] = jax.nn.sigmoid(qg[:, c:])

    def pick(t):
        r = t[(heads - 1) * quarter :]
        for h in range(heads - 2, -1, -1):
            r = jnp.where(lane_head == h, t[h * quarter : (h + 1) * quarter], r)
        return r

    def forward(kx):
        x = x_ref[0, :, :kx, :].reshape(ib * kx, c).astype(FULL)
        n = (normalize(x)[0] * g0 + g1).astype(LOW)
        n_s[: ib * kx] = n
        kv_s[: ib * kx] = dot_nn(n, wkv_ref[...]).astype(LOW)
        ones = jnp.ones((kx, c), LOW)

        def scores(i):
            qbd = block_diag(q_s[i].astype(FULL))
            return dot_nt(kv_s[i * kx : (i + 1) * kx, :c], qbd) + bias_s[:kx, :]

        def soft(s):
            return jnp.exp2(s - jnp.max(s, axis=0, keepdims=True)).astype(LOW)

        ahead = [scores(i) for i in range(min(depth, ib))]
        for i in range(ib):
            s = ahead.pop(0)
            if i + depth < ib:
                ahead.append(scores(i + depth))
            eb = soft(s)
            e_s[i * kx : (i + 1) * kx] = eb
            v = kv_s[i * kx : (i + 1) * kx, c:]
            rows = slice(i * quarter, (i + 1) * quarter)
            if omode == 0:
                o = dot_tn(eb, jnp.concatenate([v, ones], axis=1))
                o_s[rows, :] = pick(o[:, :c])
                r_s[rows, :] = 1.0 / pick(o[:, c:])
            else:
                o_s[rows, :] = compact(dot_tn(v, eb))
                total = jnp.sum(eb.astype(FULL), axis=0, keepdims=True)
                r_s[rows, :] = compact(jnp.broadcast_to(1.0 / total, (c, hj)))

    for index, kx in enumerate(variants):
        low = variants[index - 1] if index else 0

        @pl.when(jnp.logical_and(length > low, length <= kx))
        def _():
            forward(kx)

    def middle_part(t, _):
        rows = pl.ds(pl.multiple_of(t * tb, tb), tb)
        per = tb // quarter
        block = pl.ds(t * per, per)
        rinv = r_s[rows, :]
        blended = o_s[rows, :] * rinv
        gate = g_s[rows, :]
        gated = (gate * blended).astype(LOW)
        gated_s[rows, :] = gated
        mid = xq_ref[0, block].reshape(tb, c).astype(FULL) + dot_nn(gated, wo_ref[...])
        n2, spread = normalize(mid)
        shaped = (n2 * g2 + g3).astype(LOW)
        sh_s[rows, :] = shaped
        hp = dot_nn(shaped, up_ref[...])
        sg = 0.5 * jnp.tanh(0.5 * hp) + 0.5
        silu = hp * sg
        hid = silu.astype(LOW)
        hid_s[rows, :] = hid
        res_ref[0, block] = (mid + dot_nn(hid, down_ref[...])).astype(LOW).reshape(per, quarter, c)
        cot = cot_ref[0, block].reshape(tb, c)
        dh = dot_nt(cot, down_ref[...])
        dpre = (dh * (sg + silu * (1.0 - sg))).astype(LOW)
        dpre_s[rows, :] = dpre
        dsh = dot_nt(dpre, up_ref[...])
        ggain_ref[2:3, :] += jnp.sum(dsh * n2, axis=0, keepdims=True)
        ggain_ref[3:4, :] += jnp.sum(dsh, axis=0, keepdims=True)
        u = dsh * g2
        first = jnp.mean(u, axis=-1, keepdims=True)
        second = jnp.mean(u * n2, axis=-1, keepdims=True)
        dmid = cot.astype(FULL) + spread * (u - first - n2 * second)
        dml = dmid.astype(LOW)
        dml_s[rows, :] = dml
        dmid_ref[0, block] = dml.reshape(per, quarter, c)
        dgated = dot_nt(dml, wo_ref[...])
        dblend = dgated * gate
        dqg_s[rows, c:] = (dblend * blended * (1.0 - gate)).astype(LOW)
        dos = (dblend * rinv).astype(LOW)
        dos_s[block] = dos.reshape(per, quarter, c)
        xn_s[block] = (-dos.astype(FULL) * blended).astype(LOW).reshape(per, quarter, c)
        return 0

    lax.fori_loop(0, tokens // tb, middle_part, 0)
    cot_all = cot_ref[0].reshape(tokens, c)
    gdown_ref[...] += dot_tn(cot_all, hid_s[...])
    gup_ref[...] += dot_tn(sh_s[...], dpre_s[...])
    gout_ref[...] += dot_tn(gated_s[...], dml_s[...])

    def backward(kx):
        ones = jnp.ones((kx, c), LOW)

        def d_scores(i):
            dbd = block_diag(dos_s[i].astype(FULL))
            xbd = block_diag(xn_s[i].astype(FULL))
            v_one = jnp.concatenate([kv_s[i * kx : (i + 1) * kx, c:], ones], axis=1)
            return dot_nt(v_one, jnp.concatenate([dbd, xbd], axis=1)), dbd

        ahead = [d_scores(i) for i in range(min(depth, ib))]
        for i in range(ib):
            dp, dbd = ahead.pop(0)
            if i + depth < ib:
                ahead.append(d_scores(i + depth))
            span = slice(i * kx, (i + 1) * kx)
            qbd = block_diag(q_s[i].astype(FULL))
            eb = e_s[span]
            dl = eb.astype(FULL) * dp
            dbias_s[:kx, :] += dl
            dlb = dl.astype(LOW)
            dkv_s[span, c:] = dot_nn(eb, dbd).astype(LOW)
            dkv_s[span, :c] = (dot_nn(dlb, qbd) * LN2).astype(LOW)
            k = kv_s[span, :c]
            if qmode == 0:
                dq = pick(dot_tn(dlb, k))
            else:
                dq = compact(dot_tn(k, dlb))
            dqg_s[i * quarter : (i + 1) * quarter, :c] = (dq * score).astype(LOW)
        dkv = dkv_s[: ib * kx]
        gkv_ref[...] += dot_tn(n_s[: ib * kx], dkv)
        dn_s[:, :kx, :] = dot_nt(dkv, wkv_ref[...]).reshape(ib, kx, c)
        if kx < res:
            dn_s[:, kx:, :] = jnp.zeros((ib, res - kx, c), FULL)

    for index, kx in enumerate(variants):
        low = variants[index - 1] if index else 0

        @pl.when(jnp.logical_and(length > low, length <= kx))
        def _():
            backward(kx)

    own = pl.ds(pl.multiple_of(q * quarter, quarter), quarter)
    dn_s[:, own, :] += dot_nt(dqg_s[...], wqg_ref[...]).reshape(ib, quarter, c)
    y = q // 2
    k = q % 2
    for rel in range(2):
        yy = y if rel == 0 else 1 - y
        keep = pl.ds(pl.multiple_of((yy * 2 + k) * quarter, quarter), quarter)
        send = pl.ds(pl.multiple_of((yy * 2 + 1 - k) * quarter, quarter), quarter)
        (own0_ref, own1_ref)[rel][0] = dn_s[:, keep, :].astype(LOW)
        (sib0_ref, sib1_ref)[rel][0] = dn_s[:, send, :].astype(LOW)
    gqg_ref[...] += dot_tn(nq_s[...], dqg_s[...])

    @pl.when(blk == pl.num_programs(1) - 1)
    def _():
        dbias_ref[0] = dbias_s[...].T.astype(LOW)


def main_call(start, count, lengths, qidx, pair_rep, cot, bias, weights, grads, *, ib=8, variants=(128, 192, 256), tb=512, depth=2, omode=0, qmode=0, interpret=False):
    wkv, wqg, wo, up, down, gains = weights
    items, rl, res, c = pair_rep.shape
    quarter = cot.shape[2]
    hid = up.shape[1]
    heads = 4
    width = c // heads
    ib = min(ib, rl)
    tokens = ib * quarter
    hj = heads * quarter
    grid = (count, rl // ib)

    def whole(shape):
        return pl.BlockSpec(shape, lambda b, i, *_: (0,) * len(shape))

    x_spec = pl.BlockSpec((1, ib, res, c), lambda b, i, ln, q: (start + b, i, 0, 0))
    xq_spec = pl.BlockSpec((1, ib, quarter, c), lambda b, i, ln, q: (start + b, i, q[0], 0))
    cot_spec = pl.BlockSpec((1, ib, quarter, c), lambda b, i, ln, q: (start + b, i, 0, 0))
    out_q = pl.BlockSpec((1, ib, quarter, c), lambda b, i, ln, q: (b, i, 0, 0))
    bias_spec = pl.BlockSpec((1, hj, res), lambda b, i, ln, q: (b, 0, 0))
    grad_shapes = [(c, 2 * c), (c, 2 * c), (c, c), (c, hid), (c, hid), (8, c)]
    kern = functools.partial(
        main_kernel, start=start, ib=ib, heads=heads, width=width, variants=variants, tb=tb, depth=depth, omode=omode, qmode=qmode
    )
    outs = pl.pallas_call(
        kern,
        grid_spec=pltpu.PrefetchScalarGridSpec(
            num_scalar_prefetch=2,
            grid=grid,
            in_specs=[x_spec, xq_spec, cot_spec, bias_spec]
            + [whole(w.shape) for w in (wkv, wqg, wo, up, down, gains)]
            + [whole(s) for s in grad_shapes],
            out_specs=[out_q] * 6 + [bias_spec] + [whole(s) for s in grad_shapes],
            scratch_shapes=[
                pltpu.VMEM((ib * res, c), LOW),
                pltpu.VMEM((ib * res, 2 * c), LOW),
                pltpu.VMEM((ib * res, 2 * c), LOW),
                pltpu.VMEM((ib * res, hj), LOW),
                pltpu.VMEM((tokens, c), LOW),
                pltpu.VMEM((ib, quarter, c), LOW),
                pltpu.VMEM((tokens, c), FULL),
                pltpu.VMEM((tokens, c), FULL),
                pltpu.VMEM((tokens, c), FULL),
                pltpu.VMEM((ib, quarter, c), LOW),
                pltpu.VMEM((ib, quarter, c), LOW),
                pltpu.VMEM((tokens, hid), LOW),
                pltpu.VMEM((tokens, hid), LOW),
                pltpu.VMEM((tokens, c), LOW),
                pltpu.VMEM((tokens, c), LOW),
                pltpu.VMEM((tokens, c), LOW),
                pltpu.VMEM((tokens, 2 * c), LOW),
                pltpu.VMEM((res, hj), FULL),
                pltpu.VMEM((res, hj), FULL),
                pltpu.VMEM((ib, res, c), FULL),
            ],
        ),
        out_shape=[
            jax.ShapeDtypeStruct((count, rl, quarter, c), LOW)
            for _ in range(6)
        ]
        + [jax.ShapeDtypeStruct((count, hj, res), LOW)]
        + [jax.ShapeDtypeStruct(s, FULL) for s in grad_shapes],
        compiler_params=pltpu.CompilerParams(
            dimension_semantics=("arbitrary", "arbitrary"), vmem_limit_bytes=56 * 1024 * 1024
        ),
        interpret=interpret,
        name="layer",
    )(lengths, qidx, pair_rep, pair_rep, cot, bias, wkv, wqg, wo, up, down, gains, *grads)
    return outs


MOMENTUM = 0.9
AVERAGE = 0.6
RATES = (0.5, 0.3, 3.0, 0.05, 0.03, 0.1)
CHUNKS = 4


def update(weight, gradient, moment, average, step_rate, root_pairs):
    moment_next = MOMENTUM * moment + gradient
    weight_next = weight - step_rate / root_pairs * (gradient + MOMENTUM * moment_next)
    return (weight_next, moment_next, AVERAGE * average + (1.0 - AVERAGE) * weight_next)


def norm_back(d_hat, normal, spread):
    first = jnp.mean(d_hat, axis=-1, keepdims=True)
    second = jnp.mean(d_hat * normal, axis=-1, keepdims=True)
    return spread * (d_hat - first - normal * second)


def bias_kernel(q_ref, x_ref, gain_ref, bwt_ref, out_ref):
    _, rl, quarter, c = x_ref.shape
    x = x_ref[0].reshape(rl * quarter, c).astype(FULL)
    n = (normalize(x)[0] * gain_ref[0:1, :] + gain_ref[1:2, :]).astype(LOW)
    out_ref[0] = dot_nt(bwt_ref[...], n).astype(LOW)


def bias_call(qidx, pair_rep, gains, bwt, start, count, quarter):
    items, rl, res, c = pair_rep.shape
    return pl.pallas_call(
        bias_kernel,
        grid_spec=pltpu.PrefetchScalarGridSpec(
            num_scalar_prefetch=1,
            grid=(count,),
            in_specs=[
                pl.BlockSpec((1, rl, quarter, c), lambda b, q: (start + b, 0, q[0], 0)),
                pl.BlockSpec((8, c), lambda b, q: (0, 0)),
                pl.BlockSpec((8, c), lambda b, q: (0, 0)),
            ],
            out_specs=pl.BlockSpec((1, 8, rl * quarter), lambda b, q: (b, 0, 0)),
        ),
        out_shape=jax.ShapeDtypeStruct((count, 8, rl * quarter), LOW),
        compiler_params=pltpu.CompilerParams(vmem_limit_bytes=56 * 1024 * 1024),
        name="bias",
    )(qidx, pair_rep, gains, bwt)


def final_kernel(
    q_ref, x_ref, dmid_ref, own_ref, near_ref, far_ref, dbias_ref, gain_ref, bwt_ref, gin_ref, bin_ref,
    out_ref, ggain_ref, gbias_ref,
):
    _, rl, quarter, c = x_ref.shape
    tokens = rl * quarter

    @pl.when(pl.program_id(0) == 0)
    def _():
        ggain_ref[...] = gin_ref[...]
        gbias_ref[...] = bin_ref[...]

    g0 = gain_ref[0:1, :]
    normal, spread = normalize(x_ref[0].reshape(tokens, c).astype(FULL))
    normed = (normal * g0 + gain_ref[1:2, :]).astype(LOW)
    db = dbias_ref[0]
    gbias_ref[...] += dot_nn(db, normed)
    total = own_ref[0].astype(FULL) + near_ref[0].astype(FULL) + far_ref[0].astype(FULL)
    dn = total.reshape(tokens, c) + dot_tn(db, bwt_ref[...])
    ggain_ref[0:1, :] += jnp.sum(dn * normal, axis=0, keepdims=True)
    ggain_ref[1:2, :] += jnp.sum(dn, axis=0, keepdims=True)
    back = norm_back(dn * g0, normal, spread)
    out_ref[0] = (dmid_ref[0].astype(FULL) + back.reshape(rl, quarter, c)).astype(LOW)


def final_call(qidx, pair_rep, dmid, own, near, far, dbias, gains, bwt, gin, bin_, start, count):
    items, rl, res, c = pair_rep.shape
    quarter = dmid.shape[2]
    one = pl.BlockSpec((1, rl, quarter, c), lambda b, q: (b, 0, 0, 0))
    small = pl.BlockSpec((8, c), lambda b, q: (0, 0))
    return pl.pallas_call(
        final_kernel,
        grid_spec=pltpu.PrefetchScalarGridSpec(
            num_scalar_prefetch=1,
            grid=(count,),
            in_specs=[
                pl.BlockSpec((1, rl, quarter, c), lambda b, q: (start + b, 0, q[0], 0)),
                one, one, one, one,
                pl.BlockSpec((1, 8, rl * quarter), lambda b, q: (b, 0, 0)),
                small, small, small, small,
            ],
            out_specs=[one, small, small],
        ),
        out_shape=[
            jax.ShapeDtypeStruct((count, rl, quarter, c), LOW),
            jax.ShapeDtypeStruct((8, c), FULL),
            jax.ShapeDtypeStruct((8, c), FULL),
        ],
        compiler_params=pltpu.CompilerParams(vmem_limit_bytes=56 * 1024 * 1024),
        name="last",
    )(qidx, pair_rep, dmid, own, near, far, dbias, gains, bwt, gin, bin_)


def shards(
    pair_rep, lengths,
    proj_weight, bias_weight, out_weight, up_weight, down_weight, norm_gains,
    proj_moment, bias_moment, out_moment, up_moment, down_moment, gains_moment,
    proj_average, bias_average, out_average, up_average, down_average, gains_average,
    cotangent,
    *, n_rows, n_heads,
):
    both = ("rows", "heads")
    items, rl, res, c = pair_rep.shape
    quarter = cotangent.shape[2]
    hid = up_weight.shape[1]
    width = out_weight.shape[0]
    n_dev = n_rows * n_heads
    qidx = lax.axis_index("heads").astype(jnp.int32).reshape(1)
    weights = (proj_weight, bias_weight, out_weight, up_weight, down_weight, norm_gains)
    sizes = [w.size for w in weights]
    offs = [sum(sizes[:i]) for i in range(len(sizes))]
    flat = jnp.concatenate([w.astype(LOW).reshape(-1) for w in weights])
    flat = lax.all_gather(flat, both, axis=0, tiled=False)
    part = [flat[:, o : o + s] for o, s in zip(offs, sizes)]
    proj = part[0].reshape(n_rows, n_heads, c // n_rows, 4 * width).transpose(0, 2, 1, 3)
    proj = proj.reshape(c, n_heads, 4, width).transpose(2, 0, 1, 3).reshape(4, c, c)
    wkv = jnp.concatenate([proj[1], proj[2]], axis=1)
    wqg = jnp.concatenate([proj[0], proj[3]], axis=1)
    bwt = part[1].reshape(n_rows, n_heads, c // n_rows).transpose(1, 0, 2).reshape(n_heads, c)
    bwt = jnp.pad(bwt, ((0, 8 - n_heads), (0, 0)))
    wo = part[2].reshape(n_rows, n_heads, width, c // n_rows).transpose(1, 2, 0, 3).reshape(c, c)
    up = part[3].reshape(c, hid)
    down = part[4].reshape(hid, c)
    gains = part[5].reshape(n_dev, 4, c // n_dev).transpose(1, 0, 2).reshape(4, c).astype(FULL)
    gains = jnp.pad(gains, ((0, 4), (0, 0)))
    kern_weights = (wkv, wqg, wo, up, down, gains)

    group = n_rows // n_heads
    to_bias = [
        (r * n_heads + q, ((r % group) * n_heads + q) * n_heads + r // group)
        for r in range(n_rows) for q in range(n_heads)
    ]
    from_bias = [(b, a) for a, b in to_bias]
    core = [(d, d ^ 1) for d in range(n_dev)]
    cross = [(d, d ^ 2) for d in range(n_dev)]
    count = items // CHUNKS

    biases = []
    for ch in range(CHUNKS):
        piece = bias_call(qidx, pair_rep, gains, bwt, ch * count, count, quarter)
        piece = piece[:, :n_heads].reshape(count, n_heads, rl, quarter)
        piece = lax.ppermute(piece, both, to_bias)
        allb = lax.all_gather(piece, "rows", axis=0, tiled=False)
        allb = allb.reshape(group, n_heads, count, n_heads, rl, quarter).transpose(2, 3, 0, 4, 1, 5)
        biases.append(allb.reshape(count, n_heads * quarter, res))

    grads = [jnp.zeros(s, FULL) for s in [(c, 2 * c), (c, 2 * c), (c, c), (c, hid), (c, hid), (8, c)]]
    results = []
    pairs = []
    ggain = jnp.zeros((8, c), FULL)
    gbias = jnp.zeros((8, c), FULL)
    for ch in range(CHUNKS):
        outs = main_call(ch * count, count, lengths, qidx, pair_rep, cotangent, biases[ch], kern_weights, grads)
        res_c, dmid, own0, own1, sib0, sib1, dbias = outs[:7]
        grads = list(outs[7:])
        results.append(res_c)
        near1 = lax.ppermute(sib1, both, core)
        near0 = lax.ppermute(sib0, both, core)
        far = lax.ppermute((own1.astype(FULL) + near1.astype(FULL)).astype(LOW), both, cross)
        dbias = dbias.reshape(count, n_heads, group, rl, n_heads, quarter).transpose(2, 4, 0, 1, 3, 5)
        dbias = dbias.reshape(n_rows, count, n_heads, rl, quarter)
        dbias = lax.psum_scatter(dbias, "rows", scatter_dimension=0, tiled=False)
        dbias = lax.ppermute(dbias, both, from_bias)
        dbias = jnp.pad(dbias.reshape(count, n_heads, rl * quarter), ((0, 0), (0, 8 - n_heads), (0, 0)))
        dp, ggain, gbias = final_call(
            qidx, pair_rep, dmid, own0, near0, far, dbias, gains, bwt, ggain, gbias, ch * count, count
        )
        pairs.append(dp)

    gkv, gqg, gout, gup, gdown, gtwo = grads
    gproj = jnp.stack([gqg[:, :c], gkv[:, :c], gkv[:, c:], gqg[:, c:]]).reshape(4, c, n_heads, width)
    gproj = gproj.transpose(1, 2, 0, 3).reshape(n_rows, c // n_rows, n_heads, 4 * width).transpose(0, 2, 1, 3)
    gb = gbias[:n_heads].reshape(n_heads, n_rows, c // n_rows).transpose(1, 0, 2)
    go = gout.reshape(n_heads, width, n_rows, c // n_rows).transpose(2, 0, 1, 3)
    gg = jnp.concatenate([ggain[:2], gtwo[2:4]]).reshape(4, n_dev, c // n_dev).transpose(1, 0, 2)
    flat = jnp.concatenate(
        [g.reshape(n_dev, -1) for g in (gproj, gb, go, gup, gdown.T, gg)], axis=1
    )
    flat = lax.psum_scatter(flat, both, scatter_dimension=0, tiled=False)
    sums = [flat[o : o + s].reshape(w.shape) for o, s, w in zip(offs, sizes, weights)]
    moments = (proj_moment, bias_moment, out_moment, up_moment, down_moment, gains_moment)
    averages = (proj_average, bias_average, out_average, up_average, down_average, gains_average)
    root_pairs = math.sqrt(items * res * res)
    nexts = [
        update(w, g, m, a, rate, root_pairs)
        for w, g, m, a, rate in zip(weights, sums, moments, averages, RATES)
    ]
    return (
        jnp.concatenate(results, axis=0),
        jnp.concatenate(pairs, axis=0),
        *[n[0] for n in nexts],
        *[n[1] for n in nexts],
        *[n[2] for n in nexts],
    )


def solution(mesh):
    weight_specs = (
        P("rows", "heads"),
        P("rows", "heads"),
        P("heads", "rows"),
        P(("rows", "heads"), None),
        P(("rows", "heads"), None),
        P(None, ("rows", "heads")),
    )
    quarter_spec = P(None, "rows", "heads", None)
    in_specs = (P(None, "rows", None, None), P()) + weight_specs * 3 + (quarter_spec,)
    out_specs = (quarter_spec, quarter_spec) + weight_specs * 3
    body = functools.partial(shards, n_rows=mesh.shape["rows"], n_heads=mesh.shape["heads"])
    return jax.shard_map(body, mesh=mesh, in_specs=in_specs, out_specs=out_specs, check_vma=False)
```

```python
import math
import functools
import jax
import jax.numpy as jnp
from jax import lax
from jax.experimental import pallas as pl
from jax.experimental.pallas import tpu as pltpu
from jax.sharding import PartitionSpec as P

EPSILON = 1e-05
LOG2E = 1.4426950408889634
LN2 = 0.6931471805599453
LOW = jnp.bfloat16
FULL = jnp.float32


def dot_nt(a, b):
    return lax.dot_general(a, b, (((1,), (1,)), ((), ())), preferred_element_type=FULL)


def dot_nn(a, b):
    return lax.dot_general(a, b, (((1,), (0,)), ((), ())), preferred_element_type=FULL)


def dot_tn(a, b):
    return lax.dot_general(a, b, (((0,), (0,)), ((), ())), preferred_element_type=FULL)


def normalize(values):
    centre = jnp.mean(values, axis=-1, keepdims=True)
    shifted = values - centre
    spread = lax.rsqrt(jnp.mean(shifted * shifted, axis=-1, keepdims=True) + EPSILON)
    return (shifted * spread, spread)


def main_kernel(
    len_ref, q_ref,
    x_ref, xq_ref, cot_ref, bias_ref,
    wkv_ref, wqg_ref, wo_ref, up_ref, down_ref, gain_ref,
    gkv_in, gqg_in, gout_in, gup_in, gdown_in, ggain_in,
    *rest,
    start, ib, heads, width, variants, tb, depth, rl,
):
    (
        res_ref, dmid_ref, own0_ref, own1_ref, sib0_ref, sib1_ref, dbias_ref,
        gkv_ref, gqg_ref, gout_ref, gup_ref, gdown_ref, ggain_ref,
        n_s, kv_s, dkv_s, e_s, nq_s, q_s, o_s, r_s, g_s, dos_s, xn_s, hid_s, dpre_s, sh_s, dml_s, gated_s, dqg_s,
        bias_s, dbias_s, dn_s,
    ) = rest[-33:]
    item = pl.program_id(0)
    blk = pl.program_id(1)
    length = len_ref[start + item]
    q = q_ref[0]
    res = x_ref.shape[2]
    c = x_ref.shape[3]
    quarter = res // 4
    tokens = ib * quarter
    hj = heads * quarter
    score = 1.0 / math.sqrt(width)

    lane_head = lax.broadcasted_iota(jnp.int32, (1, c), 1) // width
    head_masks = [(lane_head == h).astype(FULL) for h in range(heads)]

    def block_diag(v):
        v = v.astype(FULL)
        parts = [v[g * rl : (g + 1) * rl] * m for g in range(quarter // rl) for m in head_masks]
        if rl % 16 == 0:
            return jnp.concatenate([p.astype(LOW) for p in parts], axis=0)
        return jnp.concatenate(parts, axis=0).astype(LOW)

    def pick(t):
        parts = []
        for g in range(quarter // rl):
            base = g * heads * rl
            r = t[base + (heads - 1) * rl : base + heads * rl]
            for h in range(heads - 2, -1, -1):
                r = jnp.where(lane_head == h, t[base + h * rl : base + (h + 1) * rl], r)
            parts.append(r)
        return jnp.concatenate(parts, axis=0)

    @pl.when(jnp.logical_and(item == 0, blk == 0))
    def _():
        gkv_ref[...] = gkv_in[...]
        gqg_ref[...] = gqg_in[...]
        gout_ref[...] = gout_in[...]
        gup_ref[...] = gup_in[...]
        gdown_ref[...] = gdown_in[...]
        ggain_ref[...] = ggain_in[...]

    @pl.when(blk == 0)
    def _():
        b = jnp.concatenate([bias_ref[0, g] for g in range(quarter // rl)], axis=1).astype(FULL) * LOG2E
        real = lax.broadcasted_iota(jnp.int32, (res, hj), 0) < length
        bias_s[...] = jnp.where(real, b, -1e9)
        dbias_s[...] = jnp.zeros_like(dbias_s)

    g0 = gain_ref[0:1, :]
    g1 = gain_ref[1:2, :]
    g2 = gain_ref[2:3, :]
    g3 = gain_ref[3:4, :]

    xq = xq_ref[0].reshape(tokens, c).astype(FULL)
    nq = (normalize(xq)[0] * g0 + g1).astype(LOW)
    nq_s[...] = nq
    qg = dot_nn(nq, wqg_ref[...]).astype(LOW).astype(FULL)
    q_s[...] = (qg[:, :c] * (score * LOG2E)).astype(LOW).reshape(ib, quarter, c)
    g_s[...] = jax.nn.sigmoid(qg[:, c:])

    def forward(kx):
        x = x_ref[0, :, :kx, :].reshape(ib * kx, c).astype(FULL)
        n = (normalize(x)[0] * g0 + g1).astype(LOW)
        n_s[: ib * kx] = n
        kv_s[: ib * kx] = dot_nn(n, wkv_ref[...]).astype(LOW)
        ones = jnp.ones((kx, c), LOW)

        def scores(i):
            qbd = block_diag(q_s[i])
            return dot_nt(kv_s[i * kx : (i + 1) * kx, :c], qbd) + bias_s[:kx, :]

        def soft(s):
            return jnp.exp2(s - jnp.max(s, axis=0, keepdims=True)).astype(LOW)

        ahead = [scores(i) for i in range(min(depth, ib))]
        for i in range(ib):
            s = ahead.pop(0)
            if i + depth < ib:
                ahead.append(scores(i + depth))
            eb = soft(s)
            e_s[i * kx : (i + 1) * kx] = eb
            v = kv_s[i * kx : (i + 1) * kx, c:]
            rows = slice(i * quarter, (i + 1) * quarter)
            o = dot_tn(eb, jnp.concatenate([v, ones], axis=1))
            o_s[rows, :] = pick(o[:, :c])
            r_s[rows, :] = 1.0 / pick(o[:, c:])

    for index, kx in enumerate(variants):
        low = variants[index - 1] if index else 0

        @pl.when(jnp.logical_and(length > low, length <= kx))
        def _():
            forward(kx)

    def middle_part(t, _):
        rows = pl.ds(pl.multiple_of(t * tb, tb), tb)
        per = tb // quarter
        block = pl.ds(t * per, per)
        rinv = r_s[rows, :]
        blended = o_s[rows, :] * rinv
        gate = g_s[rows, :]
        gated = (gate * blended).astype(LOW)
        gated_s[rows, :] = gated
        mid = xq_ref[0, block].reshape(tb, c).astype(FULL) + dot_nn(gated, wo_ref[...])
        n2, spread = normalize(mid)
        shaped = (n2 * g2 + g3).astype(LOW)
        sh_s[rows, :] = shaped
        hp = dot_nn(shaped, up_ref[...])
        sg = 0.5 * jnp.tanh(0.5 * hp) + 0.5
        silu = hp * sg
        hid = silu.astype(LOW)
        hid_s[rows, :] = hid
        res_ref[0, block] = (mid + dot_nn(hid, down_ref[...])).astype(LOW).reshape(per, quarter, c)
        cot = cot_ref[0, block].reshape(tb, c)
        dh = dot_nt(cot, down_ref[...])
        dpre = (dh * (sg + silu * (1.0 - sg))).astype(LOW)
        dpre_s[rows, :] = dpre
        dsh = dot_nt(dpre, up_ref[...])
        ggain_ref[2:3, :] += jnp.sum(dsh * n2, axis=0, keepdims=True)
        ggain_ref[3:4, :] += jnp.sum(dsh, axis=0, keepdims=True)
        u = dsh * g2
        first = jnp.mean(u, axis=-1, keepdims=True)
        second = jnp.mean(u * n2, axis=-1, keepdims=True)
        dmid = cot.astype(FULL) + spread * (u - first - n2 * second)
        dml = dmid.astype(LOW)
        dml_s[rows, :] = dml
        dmid_ref[0, block] = dml.reshape(per, quarter, c)
        dgated = dot_nt(dml, wo_ref[...])
        dblend = dgated * gate
        dqg_s[rows, c:] = (dblend * blended * (1.0 - gate)).astype(LOW)
        dos = (dblend * rinv).astype(LOW)
        dos_s[block] = dos.reshape(per, quarter, c)
        xn_s[block] = (-dos.astype(FULL) * blended).astype(LOW).reshape(per, quarter, c)
        return 0

    lax.fori_loop(0, tokens // tb, middle_part, 0)
    cot_all = cot_ref[0].reshape(tokens, c)
    gdown_ref[...] += dot_tn(cot_all, hid_s[...])
    gup_ref[...] += dot_tn(sh_s[...], dpre_s[...])
    gout_ref[...] += dot_tn(gated_s[...], dml_s[...])

    def backward(kx):
        ones = jnp.ones((kx, c), LOW)

        def d_scores(i):
            dbd = block_diag(dos_s[i])
            xbd = block_diag(xn_s[i])
            v_one = jnp.concatenate([kv_s[i * kx : (i + 1) * kx, c:], ones], axis=1)
            return dot_nt(v_one, jnp.concatenate([dbd, xbd], axis=1)), dbd

        ahead = [d_scores(i) for i in range(min(depth, ib))]
        for i in range(ib):
            dp, dbd = ahead.pop(0)
            if i + depth < ib:
                ahead.append(d_scores(i + depth))
            span = slice(i * kx, (i + 1) * kx)
            qbd = block_diag(q_s[i])
            eb = e_s[span]
            dl = eb.astype(FULL) * dp
            dbias_s[:kx, :] += dl
            dlb = dl.astype(LOW)
            dkv_s[span, c:] = dot_nn(eb, dbd).astype(LOW)
            dkv_s[span, :c] = (dot_nn(dlb, qbd) * LN2).astype(LOW)
            k = kv_s[span, :c]
            dq = pick(dot_tn(dlb, k))
            dqg_s[i * quarter : (i + 1) * quarter, :c] = (dq * score).astype(LOW)
        dkv = dkv_s[: ib * kx]
        gkv_ref[...] += dot_tn(n_s[: ib * kx], dkv)
        dn_s[:, :kx, :] = dot_nt(dkv, wkv_ref[...]).reshape(ib, kx, c)
        if kx < res:
            dn_s[:, kx:, :] = jnp.zeros((ib, res - kx, c), FULL)

    for index, kx in enumerate(variants):
        low = variants[index - 1] if index else 0

        @pl.when(jnp.logical_and(length > low, length <= kx))
        def _():
            backward(kx)

    own = pl.ds(pl.multiple_of(q * quarter, quarter), quarter)
    dn_s[:, own, :] += dot_nt(dqg_s[...], wqg_ref[...]).reshape(ib, quarter, c)
    y = q // 2
    k = q % 2
    for rel in range(2):
        yy = y if rel == 0 else 1 - y
        keep = pl.ds(pl.multiple_of((yy * 2 + k) * quarter, quarter), quarter)
        send = pl.ds(pl.multiple_of((yy * 2 + 1 - k) * quarter, quarter), quarter)
        (own0_ref, own1_ref)[rel][0] = dn_s[:, keep, :].astype(LOW)
        (sib0_ref, sib1_ref)[rel][0] = dn_s[:, send, :].astype(LOW)
    gqg_ref[...] += dot_tn(nq_s[...], dqg_s[...])

    @pl.when(blk == pl.num_programs(1) - 1)
    def _():
        for g in range(quarter // rl):
            dbias_ref[0, g] = dbias_s[:, g * heads * rl : (g + 1) * heads * rl].astype(LOW)


def main_call(start, count, lengths, qidx, pair_rep, cot, bias, weights, grads, carried=(), after=(), *, ib=8, variants=(128, 192, 256), tb=512, depth=2):
    wkv, wqg, wo, up, down, gains = weights
    items, rl, res, c = pair_rep.shape
    quarter = cot.shape[2]
    hid = up.shape[1]
    heads = 4
    width = c // heads
    ib = min(ib, rl)
    tokens = ib * quarter
    hj = heads * quarter
    grid = (count, rl // ib)

    def whole(shape):
        return pl.BlockSpec(shape, lambda b, i, *_: (0,) * len(shape))

    x_spec = pl.BlockSpec((1, ib, res, c), lambda b, i, ln, q: (start + b, i, 0, 0))
    xq_spec = pl.BlockSpec((1, ib, quarter, c), lambda b, i, ln, q: (start + b, i, q[0], 0))
    cot_spec = pl.BlockSpec((1, ib, quarter, c), lambda b, i, ln, q: (start + b, i, 0, 0))
    out_q = pl.BlockSpec((1, ib, quarter, c), lambda b, i, ln, q: (b, i, 0, 0))
    bias_spec = pl.BlockSpec((1,) + bias.shape[1:], lambda b, i, ln, q: (start + b, 0, 0, 0))
    grad_shapes = [(c, 2 * c), (c, 2 * c), (c, c), (c, hid), (c, hid), (8, c)]
    kern = functools.partial(
        main_kernel, start=start, ib=ib, heads=heads, width=width, variants=variants, tb=tb, depth=depth, rl=rl
    )
    any_spec = pl.BlockSpec(memory_space=pl.ANY)
    part = jax.ShapeDtypeStruct((count, rl, quarter, c), LOW)
    return pl.pallas_call(
        kern,
        grid_spec=pltpu.PrefetchScalarGridSpec(
            num_scalar_prefetch=2,
            grid=grid,
            in_specs=[x_spec, xq_spec, cot_spec, bias_spec]
            + [whole(w.shape) for w in weights]
            + [whole(s) for s in grad_shapes]
            + [any_spec] * (len(carried) + len(after)),
            out_specs=[cot_spec] + [out_q] * 5 + [bias_spec] + [whole(s) for s in grad_shapes],
            scratch_shapes=[
                pltpu.VMEM((ib * res, c), LOW),
                pltpu.VMEM((ib * res, 2 * c), LOW),
                pltpu.VMEM((ib * res, 2 * c), LOW),
                pltpu.VMEM((ib * res, hj), LOW),
                pltpu.VMEM((tokens, c), LOW),
                pltpu.VMEM((ib, quarter, c), LOW),
                pltpu.VMEM((tokens, c), FULL),
                pltpu.VMEM((tokens, c), FULL),
                pltpu.VMEM((tokens, c), FULL),
                pltpu.VMEM((ib, quarter, c), LOW),
                pltpu.VMEM((ib, quarter, c), LOW),
                pltpu.VMEM((tokens, hid), LOW),
                pltpu.VMEM((tokens, hid), LOW),
                pltpu.VMEM((tokens, c), LOW),
                pltpu.VMEM((tokens, c), LOW),
                pltpu.VMEM((tokens, c), LOW),
                pltpu.VMEM((tokens, 2 * c), LOW),
                pltpu.VMEM((res, hj), FULL),
                pltpu.VMEM((res, hj), FULL),
                pltpu.VMEM((ib, res, c), FULL),
            ],
        ),
        out_shape=[jax.ShapeDtypeStruct((items, rl, quarter, c), LOW)]
        + [part] * 5
        + [jax.ShapeDtypeStruct(bias.shape, LOW)]
        + [jax.ShapeDtypeStruct(s, FULL) for s in grad_shapes],
        input_output_aliases={18: 0, 19: 6} if carried else {},
        compiler_params=pltpu.CompilerParams(
            dimension_semantics=("arbitrary", "arbitrary"), vmem_limit_bytes=56 * 1024 * 1024
        ),
        cost_estimate=pl.CostEstimate(
            flops=60_000_000 * count * rl * 8, bytes_accessed=2_000_000 * count * rl // 8, transcendentals=0
        ),
        name="layer",
    )(lengths, qidx, pair_rep, pair_rep, cot, bias, *weights, *grads, *carried, *after)


MESH = pl.DeviceIdType.MESH
MOMENTUM = 0.9
AVERAGE = 0.6
RATES = (0.5, 0.3, 3.0, 0.05, 0.03, 0.1)
CHUNKS = (4, 3, 3, 2)


def pad16(n):
    return -(-n // 16) * 16


def greet_all(n_dev, n_heads, me):
    barrier = pltpu.get_barrier_semaphore()

    def signal(s, _):
        d = lax.rem(me + s, n_dev)
        pl.semaphore_signal(barrier, inc=1, device_id=(d // n_heads, lax.rem(d, n_heads)), device_id_type=MESH)
        return 0

    lax.fori_loop(1, n_dev, signal, 0)
    pl.semaphore_wait(barrier, n_dev - 1)


def prep_kernel(
    x_hbm, proj_ref, bw_ref, out_ref, up_ref, down_ref, gains_ref,
    wkv_ref, wqg_ref, wo_ref, upall_ref, downall_ref, gainall_ref, base_ref, bias_hbm,
    stage, wbuf, proj_s, up_s, down_s, base_s, stack_ref, xbuf, xhat, pbuf,
    x_sem, wsend, wrecv, bsend, brecv, self_sem,
    *, n_rows, n_heads, parts,
):
    items, rl, res, c = x_hbm.shape
    hid = up_ref.shape[1]
    quarter = res // n_heads
    width = out_ref.shape[0]
    n_dev = n_rows * n_heads
    group = n_rows // n_heads
    lanes = n_heads * rl
    r = lax.axis_index("rows")
    q = lax.axis_index("heads")
    me = r * n_heads + q

    def load(b):
        span = pl.ds(pl.multiple_of(q * quarter, quarter), quarter)
        return pltpu.make_async_copy(x_hbm.at[b, :, span, :], xbuf.at[b], x_sem.at[b])

    for b in range(items):
        load(b).start()

    pr, ur, dr, cr, cd = c // n_rows, c // n_dev, hid // n_dev, c // n_rows, c // n_dev
    o_down = pad16(pr)
    o_up = o_down + pad16(dr)
    o_out = o_up + pad16(ur * (hid // c))
    o_gain = o_out + pad16(width)
    o_bias = o_gain + 16
    lane = lax.broadcasted_iota(jnp.int32, (1, c), 1)
    stage[...] = jnp.zeros_like(stage)
    stage[:pr, :] = proj_ref[...]
    stage[o_down : o_down + dr, :] = down_ref[...]
    for g in range(hid // c):
        stage[o_up + g * ur : o_up + (g + 1) * ur, :] = up_ref[:, g * c : (g + 1) * c]
    placed = jnp.zeros((width, c), FULL)
    for i in range(cr):
        placed = placed + jnp.where(lane == r * cr + i, out_ref[:, i : i + 1], 0.0)
    stage[o_out : o_out + width, :] = placed
    placed = jnp.zeros((4, c), FULL)
    for i in range(cd):
        placed = placed + jnp.where(lane == me * cd + i, gains_ref[:, i : i + 1], 0.0)
    stage[o_gain : o_gain + 4, :] = placed
    stage[o_bias : o_bias + pr, :] = jnp.where(lane // rl == q, bw_ref[...], 0.0)
    wbuf[me] = stage[...].astype(LOW)

    greet_all(n_dev, n_heads, me)

    def weights_to(s):
        d = lax.rem(me + s, n_dev)
        return pltpu.make_async_remote_copy(
            src_ref=wbuf.at[me],
            dst_ref=wbuf.at[me],
            send_sem=wsend.at[s],
            recv_sem=wrecv.at[s],
            device_id=(d // n_heads, lax.rem(d, n_heads)),
            device_id_type=MESH,
        )

    def start_one(s, _):
        weights_to(s).start()
        return 0

    lax.fori_loop(1, n_dev, start_one, 0)

    for b in range(items):
        load(b).wait()
        xhat[b] = normalize(xbuf[b].reshape(rl * quarter, c).astype(FULL))[0]

    def wait_one(s, _):
        weights_to(s).wait()
        return 0

    lax.fori_loop(1, n_dev, wait_one, 0)

    gain_sum = jnp.zeros((16, c), FULL)
    for h in range(n_heads):
        whole = jnp.zeros((width, c), FULL)
        for rr in range(n_rows):
            d = rr * n_heads + h
            proj_s[rr * pr : (rr + 1) * pr, h * c : (h + 1) * c] = wbuf[d, :pr].astype(FULL)
            whole = whole + wbuf[d, o_out : o_out + width].astype(FULL)
        wo_ref[h * width : (h + 1) * width, :] = whole.astype(LOW)
    for d in range(n_dev):
        down_s[d * dr : (d + 1) * dr, :] = wbuf[d, o_down : o_down + dr].astype(FULL)
        for g in range(hid // c):
            up_s[d * ur : (d + 1) * ur, g * c : (g + 1) * c] = wbuf[d, o_up + g * ur : o_up + (g + 1) * ur].astype(FULL)
        gain_sum = gain_sum + wbuf[d, o_gain : o_gain + 16].astype(FULL)
    for rr in range(n_rows):
        total = jnp.zeros((pr, c), FULL)
        for h in range(n_heads):
            total = total + wbuf[rr * n_heads + h, o_bias : o_bias + pr].astype(FULL)
        base_s[rr * pr : (rr + 1) * pr, :] = total
    downall_ref[...] = down_s[...].astype(LOW)
    upall_ref[...] = up_s[...].astype(LOW)
    gainall_ref[...] = gain_sum[:8]
    src = lax.broadcasted_iota(jnp.int32, (n_heads * c, 2 * c), 0)
    dst = lax.broadcasted_iota(jnp.int32, (n_heads * c, 2 * c), 1)
    place = (lax.rem(dst, c) // width) * c + lax.rem(dst, width)
    second = dst // c
    proj_low = proj_s[...].astype(LOW)
    wqg_ref[...] = dot_nn(proj_low, (src == place + second * 3 * width).astype(LOW)).astype(LOW)
    wkv_ref[...] = dot_nn(proj_low, (src == place + width + second * width).astype(LOW)).astype(LOW)
    base = base_s[...]
    base_ref[...] = base[:, :lanes].astype(LOW)
    for jj in range(rl):
        stack_ref[jj * c : (jj + 1) * c, :] = jnp.where(lax.rem(lane, rl) == jj, base, 0.0)[:, :lanes].astype(LOW)

    g0 = gain_sum[0:1]
    g1 = gain_sum[1:2]
    target = r // group
    slot = lax.rem(r, group)
    span = pl.ds(pl.multiple_of(q * quarter, quarter), quarter)
    size = items // parts

    def own_copy(p):
        return pltpu.make_async_copy(
            pbuf.at[pl.ds(p * size, size)], bias_hbm.at[pl.ds(p * size, size), slot, span, :], self_sem.at[p]
        )

    def bias_to(p, t, s):
        return pltpu.make_async_remote_copy(
            src_ref=pbuf.at[pl.ds(p * size, size)],
            dst_ref=bias_hbm.at[pl.ds(p * size, size), slot, span, :],
            send_sem=bsend.at[p, t],
            recv_sem=brecv.at[p, s],
            device_id=(t, target),
            device_id_type=MESH,
        )

    mine = slot * n_heads + q
    for p in range(parts):

        def piece(b, _):
            n = (xhat[b] * g0 + g1).astype(LOW).reshape(rl, quarter, c)
            wide = jnp.concatenate([n[jj] for jj in range(rl)], axis=1)
            pbuf[b] = dot_nn(wide, stack_ref[...]).astype(LOW)
            return 0

        lax.fori_loop(p * size, (p + 1) * size, piece, 0)

        def send(t, _):
            is_me = jnp.logical_and(t == r, target == q)

            @pl.when(is_me)
            def _():
                own_copy(p).start()

            @pl.when(jnp.logical_not(is_me))
            def _():
                bias_to(p, t, mine).start()

            return 0

        lax.fori_loop(0, n_rows, send, 0)

    for p in range(parts):

        def finish(t, _):
            is_me = jnp.logical_and(t == r, target == q)

            @pl.when(is_me)
            def _():
                own_copy(p).wait()

            @pl.when(jnp.logical_not(is_me))
            def _():
                bias_to(p, t, mine).wait_send()

            from_me = jnp.logical_and(q * group + t // n_heads == r, lax.rem(t, n_heads) == q)

            @pl.when(jnp.logical_not(from_me))
            def _():
                bias_to(p, t, t).wait_recv()

            return 0

        lax.fori_loop(0, n_rows, finish, 0)


def prep_call(pair_rep, weights, n_rows, n_heads, quarter, parts=3):
    items, rl, res, c = pair_rep.shape
    proj, bw, out, up, down, gains = weights
    hid = up.shape[1]
    n_dev = n_rows * n_heads
    group = n_rows // n_heads
    lanes = n_heads * rl
    width = out.shape[0]
    rows = pad16(c // n_rows) + pad16(hid // n_dev) + pad16(c // n_dev * (hid // c)) + pad16(width) + 16 + pad16(c // n_rows)
    vmem = pl.BlockSpec(memory_space=pltpu.VMEM)
    hbm = pl.BlockSpec(memory_space=pl.ANY)
    return pl.pallas_call(
        functools.partial(prep_kernel, n_rows=n_rows, n_heads=n_heads, parts=parts),
        in_specs=[hbm] + [vmem] * 6,
        out_specs=[vmem] * 7 + [hbm],
        out_shape=[
            jax.ShapeDtypeStruct((c, 2 * c), LOW),
            jax.ShapeDtypeStruct((c, 2 * c), LOW),
            jax.ShapeDtypeStruct((c, c), LOW),
            jax.ShapeDtypeStruct((c, hid), LOW),
            jax.ShapeDtypeStruct((hid, c), LOW),
            jax.ShapeDtypeStruct((8, c), FULL),
            jax.ShapeDtypeStruct((c, lanes), LOW),
            jax.ShapeDtypeStruct((items, group, res, lanes), LOW),
        ],
        scratch_shapes=[
            pltpu.VMEM((rows, c), FULL),
            pltpu.VMEM((n_dev, rows, c), LOW),
            pltpu.VMEM((c, n_heads * c), FULL),
            pltpu.VMEM((c, hid), FULL),
            pltpu.VMEM((hid, c), FULL),
            pltpu.VMEM((c, c), FULL),
            pltpu.VMEM((rl * c, lanes), LOW),
            pltpu.VMEM((items, rl, quarter, c), LOW),
            pltpu.VMEM((items, rl * quarter, c), FULL),
            pltpu.VMEM((items, quarter, lanes), LOW),
            pltpu.SemaphoreType.DMA((items,)),
            pltpu.SemaphoreType.DMA((n_dev,)),
            pltpu.SemaphoreType.DMA((n_dev,)),
            pltpu.SemaphoreType.DMA((parts, n_rows)),
            pltpu.SemaphoreType.DMA((parts, n_rows)),
            pltpu.SemaphoreType.DMA((parts,)),
        ],
        compiler_params=pltpu.CompilerParams(
            collective_id=0, has_side_effects=True, vmem_limit_bytes=56 * 1024 * 1024
        ),
        name="prep",
    )(pair_rep, *weights)


def gather_kernel(
    grads_hbm, dbias_hbm, near_hbm, far_hbm, diagonal_hbm, sums_ref, db_ref,
    gbuf, dbuf, gsend, grecv, dsend, drecv, self_sem,
    *, n_rows, n_heads,
):
    n_dev = n_rows * n_heads
    group = n_rows // n_heads
    items, _, res, lanes = dbias_hbm.shape
    quarter = res // n_heads
    r = lax.axis_index("rows")
    q = lax.axis_index("heads")
    me = r * n_heads + q
    greet_all(n_dev, n_heads, me)

    def db_src(g, h):
        return dbias_hbm.at[:, g, pl.ds(pl.multiple_of(h * quarter, quarter), quarter), :]

    def db_to(t):
        g, h = t // n_heads, lax.rem(t, n_heads)
        return pltpu.make_async_remote_copy(
            src_ref=db_src(g, h),
            dst_ref=dbuf.at[r],
            send_sem=dsend.at[t],
            recv_sem=drecv.at[r],
            device_id=(q * group + g, h),
            device_id_type=MESH,
        )

    def db_from(t):
        return pltpu.make_async_remote_copy(
            src_ref=dbuf.at[t],
            dst_ref=dbuf.at[t],
            send_sem=dsend.at[t],
            recv_sem=drecv.at[t],
            device_id=(t, q),
            device_id_type=MESH,
        )

    def db_own(t):
        return pltpu.make_async_copy(db_src(t // n_heads, lax.rem(t, n_heads)), dbuf.at[r], self_sem.at[0])

    def is_me(t):
        return jnp.logical_and(q * group + t // n_heads == r, lax.rem(t, n_heads) == q)

    def from_me(t):
        return jnp.logical_and(t == r, r // group == q)

    def db_start(t, _):
        @pl.when(is_me(t))
        def _():
            db_own(t).start()

        @pl.when(jnp.logical_not(is_me(t)))
        def _():
            db_to(t).start()

        return 0

    lax.fori_loop(0, n_rows, db_start, 0)

    def grad_to(s):
        d = lax.rem(me + s, n_dev)
        return pltpu.make_async_remote_copy(
            src_ref=grads_hbm.at[d],
            dst_ref=gbuf.at[me],
            send_sem=gsend.at[s],
            recv_sem=grecv.at[s],
            device_id=(d // n_heads, lax.rem(d, n_heads)),
            device_id_type=MESH,
        )

    def grad_start(s, _):
        grad_to(s).start()
        return 0

    lax.fori_loop(1, n_dev, grad_start, 0)
    own = pltpu.make_async_copy(grads_hbm.at[me], gbuf.at[me], self_sem.at[1])
    own.start()
    own.wait()

    def grad_wait(s, _):
        grad_to(s).wait()
        return 0

    lax.fori_loop(1, n_dev, grad_wait, 0)

    def grad_add(d, total):
        return total + gbuf[d].astype(FULL)

    sums_ref[...] = lax.fori_loop(0, n_dev, grad_add, jnp.zeros(sums_ref.shape, FULL))

    def db_wait(t, _):
        @pl.when(is_me(t))
        def _():
            db_own(t).wait()

        @pl.when(jnp.logical_not(is_me(t)))
        def _():
            db_to(t).wait_send()

        @pl.when(jnp.logical_not(from_me(t)))
        def _():
            db_from(t).wait_recv()

        return 0

    lax.fori_loop(0, n_rows, db_wait, 0)

    def db_add(b, _):
        total = jnp.zeros((quarter, lanes), FULL)
        for t in range(n_rows):
            total = total + dbuf[t, b].astype(FULL)
        db_ref[b] = total.astype(LOW)
        return 0

    lax.fori_loop(0, items, db_add, 0)


def gather_call(grads, dbias, after, n_rows, n_heads):
    n_dev = n_rows * n_heads
    items, group, res, lanes = dbias.shape
    quarter = res // n_heads
    rows, c = grads.shape[1:]
    vmem = pl.BlockSpec(memory_space=pltpu.VMEM)
    hbm = pl.BlockSpec(memory_space=pl.ANY)
    return pl.pallas_call(
        functools.partial(gather_kernel, n_rows=n_rows, n_heads=n_heads),
        in_specs=[hbm] * 5,
        out_specs=[vmem, vmem],
        out_shape=[
            jax.ShapeDtypeStruct((rows, c), FULL),
            jax.ShapeDtypeStruct((items, quarter, lanes), LOW),
        ],
        scratch_shapes=[
            pltpu.VMEM((n_dev, rows, c), LOW),
            pltpu.VMEM((n_rows, items, quarter, lanes), LOW),
            pltpu.SemaphoreType.DMA((n_dev,)),
            pltpu.SemaphoreType.DMA((n_dev,)),
            pltpu.SemaphoreType.DMA((n_rows,)),
            pltpu.SemaphoreType.DMA((n_rows,)),
            pltpu.SemaphoreType.DMA((2,)),
        ],
        compiler_params=pltpu.CompilerParams(
            collective_id=1, has_side_effects=True, vmem_limit_bytes=56 * 1024 * 1024
        ),
        name="gather",
    )(grads, dbias, *after)


def small_kernel(ggain_ref, gbias_ref, sums_ref, buf, send_sem, recv_sem, *, n_rows, n_heads):
    n_dev = n_rows * n_heads
    lanes = gbias_ref.shape[1]
    rl = lanes // n_heads
    r = lax.axis_index("rows")
    q = lax.axis_index("heads")
    me = r * n_heads + q
    heads = lax.broadcasted_iota(jnp.int32, (8, lanes), 0) - 2
    sel = (lax.broadcasted_iota(jnp.int32, (8, lanes), 1) // rl == heads).astype(FULL)
    rows = lax.dot_general(
        sel, gbias_ref[...], (((1,), (1,)), ((), ())), precision=lax.Precision.HIGHEST, preferred_element_type=FULL
    )
    row = lax.broadcasted_iota(jnp.int32, ggain_ref.shape, 0)
    buf[me] = jnp.where(row < 2, ggain_ref[...], rows)
    greet_all(n_dev, n_heads, me)

    def copy_to(s):
        d = lax.rem(me + s, n_dev)
        return pltpu.make_async_remote_copy(
            src_ref=buf.at[me],
            dst_ref=buf.at[me],
            send_sem=send_sem.at[s],
            recv_sem=recv_sem.at[s],
            device_id=(d // n_heads, lax.rem(d, n_heads)),
            device_id_type=MESH,
        )

    def start_one(s, _):
        copy_to(s).start()
        return 0

    def wait_one(s, _):
        copy_to(s).wait()
        return 0

    lax.fori_loop(1, n_dev, start_one, 0)
    lax.fori_loop(1, n_dev, wait_one, 0)
    sums_ref[...] = lax.fori_loop(0, n_dev, lambda d, t: t + buf[d], jnp.zeros(sums_ref.shape, FULL))


def small_call(ggain, gbias, n_rows, n_heads):
    n_dev = n_rows * n_heads
    vmem = pl.BlockSpec(memory_space=pltpu.VMEM)
    return pl.pallas_call(
        functools.partial(small_kernel, n_rows=n_rows, n_heads=n_heads),
        in_specs=[vmem, vmem],
        out_specs=vmem,
        out_shape=jax.ShapeDtypeStruct(ggain.shape, FULL),
        scratch_shapes=[
            pltpu.VMEM((n_dev,) + ggain.shape, FULL),
            pltpu.SemaphoreType.DMA((n_dev,)),
            pltpu.SemaphoreType.DMA((n_dev,)),
        ],
        compiler_params=pltpu.CompilerParams(collective_id=2, has_side_effects=True),
        name="small",
    )(ggain, gbias)


def norm_back(d_hat, normal, spread):
    first = jnp.mean(d_hat, axis=-1, keepdims=True)
    second = jnp.mean(d_hat * normal, axis=-1, keepdims=True)
    return spread * (d_hat - first - normal * second)


def final_kernel(
    q_ref, x_ref, dmid_ref, own_ref, a_ref, b_ref, c_ref, db_ref, gain_ref, base_ref, gin_ref, bin_ref, *rest,
):
    out_ref, ggain_ref, gbias_ref = rest[-3:]
    _, rl, quarter, c = x_ref.shape
    tokens = rl * quarter
    lanes = db_ref.shape[2]

    @pl.when(pl.program_id(0) == 0)
    def _():
        ggain_ref[...] = gin_ref[...]
        gbias_ref[...] = bin_ref[...]

    g0 = gain_ref[0:1, :]
    normal, spread = normalize(x_ref[0].reshape(tokens, c).astype(FULL))
    normed = (normal * g0 + gain_ref[1:2, :]).astype(LOW)
    db = db_ref[0]
    lane = lax.rem(lax.broadcasted_iota(jnp.int32, (1, lanes), 1), rl)
    spread_db = jnp.concatenate([jnp.where(lane == jj, db, jnp.zeros_like(db)) for jj in range(rl)], axis=0)
    gbias_ref[...] += dot_tn(normed, spread_db)
    total = own_ref[0].astype(FULL) + a_ref[0].astype(FULL) + b_ref[0].astype(FULL) + c_ref[0].astype(FULL)
    dn = total.reshape(tokens, c) + dot_nt(spread_db, base_ref[...])
    ggain_ref[0:1, :] += jnp.sum(dn * normal, axis=0, keepdims=True)
    ggain_ref[1:2, :] += jnp.sum(dn, axis=0, keepdims=True)
    back = norm_back(dn * g0, normal, spread)
    out_ref[0] = (dmid_ref[0].astype(FULL) + back.reshape(rl, quarter, c)).astype(LOW)


def final_call(qidx, pair_rep, terms, db, gains, base, sums, start, carried=()):
    items, rl, res, c = pair_rep.shape
    count, _, quarter, _ = terms[0].shape
    lanes = db.shape[2]
    one = pl.BlockSpec((1, rl, quarter, c), lambda b, q: (b, 0, 0, 0))
    small = pl.BlockSpec((8, c), lambda b, q: (0, 0))
    wide = pl.BlockSpec((c, lanes), lambda b, q: (0, 0))
    return pl.pallas_call(
        final_kernel,
        grid_spec=pltpu.PrefetchScalarGridSpec(
            num_scalar_prefetch=1,
            grid=(count,),
            in_specs=[pl.BlockSpec((1, rl, quarter, c), lambda b, q: (start + b, 0, q[0], 0))]
            + [one] * 5
            + [pl.BlockSpec((1, quarter, lanes), lambda b, q: (start + b, 0, 0)), small]
            + [wide, small, wide]
            + [pl.BlockSpec(memory_space=pl.ANY)] * len(carried),
            out_specs=[pl.BlockSpec((1, rl, quarter, c), lambda b, q: (start + b, 0, 0, 0)), small, wide],
        ),
        out_shape=[
            jax.ShapeDtypeStruct((items, rl, quarter, c), LOW),
            jax.ShapeDtypeStruct((8, c), FULL),
            jax.ShapeDtypeStruct((c, lanes), FULL),
        ],
        input_output_aliases={12: 0} if carried else {},
        compiler_params=pltpu.CompilerParams(vmem_limit_bytes=56 * 1024 * 1024),
        name="last",
    )(qidx, pair_rep, *terms, db, gains, base, *sums, *carried)


def update(weight, gradient, moment, average, step_rate, root_pairs):
    moment_next = MOMENTUM * moment + gradient
    weight_next = weight - step_rate / root_pairs * (gradient + MOMENTUM * moment_next)
    return (weight_next, moment_next, AVERAGE * average + (1.0 - AVERAGE) * weight_next)


def shards(
    pair_rep, lengths,
    proj_weight, bias_weight, out_weight, up_weight, down_weight, norm_gains,
    proj_moment, bias_moment, out_moment, up_moment, down_moment, gains_moment,
    proj_average, bias_average, out_average, up_average, down_average, gains_average,
    cotangent,
    *, n_rows, n_heads,
):
    both = ("rows", "heads")
    items, rl, res, c = pair_rep.shape
    quarter = cotangent.shape[2]
    hid = up_weight.shape[1]
    width = out_weight.shape[0]
    n_dev = n_rows * n_heads
    q = lax.axis_index("heads").astype(jnp.int32)
    r = lax.axis_index("rows").astype(jnp.int32)
    qidx = q.reshape(1)
    weights = (proj_weight, bias_weight, out_weight, up_weight, down_weight, norm_gains)
    wkv, wqg, wo, up, down, gains, base, bias = prep_call(pair_rep, weights, n_rows, n_heads, quarter)

    core = [(d, d ^ 1) for d in range(n_dev)]
    cross = [(d, d ^ 2) for d in range(n_dev)]
    both_moved = [(d, d ^ 3) for d in range(n_dev)]

    grads = [jnp.zeros(s, FULL) for s in [(c, 2 * c), (c, 2 * c), (c, c), (c, hid), (c, hid), (8, c)]]
    carried = ()
    terms = []
    start = 0
    for count in CHUNKS:
        outs = main_call(
            start, count, lengths, qidx, pair_rep, cotangent, bias, (wkv, wqg, wo, up, down, gains), grads, carried,
            terms[-2][1][2:] if len(terms) > 1 else (),
        )
        result, dmid, own0, own1, sib0, sib1, dbias = outs[:7]
        grads = list(outs[7:])
        carried = (result, dbias)
        far = lax.ppermute(own1, both, cross)
        diagonal = lax.ppermute(sib1, both, both_moved)
        near = lax.ppermute(sib0, both, core)
        terms.append((start, (dmid, own0, near, far, diagonal)))
        start += count

    gkv, gqg, gout, gup, gdown, gtwo = grads
    gproj = jnp.stack([gqg[:, :c], gkv[:, :c], gkv[:, c:], gqg[:, c:]]).reshape(4, c, n_heads, width)
    gproj = gproj.transpose(1, 2, 0, 3).reshape(n_rows, c // n_rows, n_heads, 4 * width).transpose(0, 2, 1, 3)
    go = gout.reshape(n_heads, width, n_rows, c // n_rows).transpose(2, 0, 1, 3)
    gg = gtwo[2:4].reshape(2, n_dev, c // n_dev).transpose(1, 0, 2)
    flat = [g.reshape(n_dev, -1).astype(LOW) for g in (gproj, go, gup, gdown.T, gg)]
    sizes = [g.shape[1] for g in flat]
    offs = [sum(sizes[:i]) for i in range(len(sizes))]
    full = -(-sum(sizes) // (16 * c)) * 16 * c
    flat = jnp.pad(jnp.concatenate(flat, axis=1), ((0, 0), (0, full - sum(sizes))))
    flat, db = gather_call(flat.reshape(n_dev, full // c, c), dbias, terms[-2][1][2:], n_rows, n_heads)
    flat = flat.reshape(-1)
    s_proj, s_out, s_up, s_down, s_two = [flat[o : o + s] for o, s in zip(offs, sizes)]

    sums = (jnp.zeros((8, c), FULL), jnp.zeros((c, n_heads * rl), FULL))
    done = ()
    for start, parts in terms:
        d_pair, *sums = final_call(qidx, pair_rep, parts, db, gains, base, sums, start, done)
        done = (d_pair,)
    small = small_call(*sums, n_rows, n_heads)
    cd, cr = c // n_dev, c // n_rows
    s_one = lax.dynamic_slice(small, (0, (r * n_heads + q) * cd), (2, cd))
    s_bias = lax.dynamic_slice(small, (2 + q, r * cr), (1, cr)).reshape(cr, 1)
    s_gains = jnp.concatenate([s_one, s_two.reshape(2, cd)])
    sums = (s_proj, s_bias, s_out, s_up, s_down, s_gains)
    moments = (proj_moment, bias_moment, out_moment, up_moment, down_moment, gains_moment)
    averages = (proj_average, bias_average, out_average, up_average, down_average, gains_average)
    root_pairs = math.sqrt(items * res * res)
    nexts = [
        update(w, g.reshape(w.shape), m, a, rate, root_pairs)
        for w, g, m, a, rate in zip(weights, sums, moments, averages, RATES)
    ]
    return (
        result,
        d_pair,
        *[n[0] for n in nexts],
        *[n[1] for n in nexts],
        *[n[2] for n in nexts],
    )


def solution(mesh):
    weight_specs = (
        P("rows", "heads"),
        P("rows", "heads"),
        P("heads", "rows"),
        P(("rows", "heads"), None),
        P(("rows", "heads"), None),
        P(None, ("rows", "heads")),
    )
    quarter_spec = P(None, "rows", "heads", None)
    in_specs = (P(None, "rows", None, None), P()) + weight_specs * 3 + (quarter_spec,)
    out_specs = (quarter_spec, quarter_spec) + weight_specs * 3
    body = functools.partial(shards, n_rows=mesh.shape["rows"], n_heads=mesh.shape["heads"])
    return jax.shard_map(body, mesh=mesh, in_specs=in_specs, out_specs=out_specs, check_vma=False)
```

```python
import math
import functools
import jax
import jax.numpy as jnp
from jax import lax
from jax.experimental import pallas as pl
from jax.experimental.pallas import tpu as pltpu
from jax.sharding import PartitionSpec as P

EPSILON = 1e-05
LOG2E = 1.4426950408889634
LN2 = 0.6931471805599453
LOW = jnp.bfloat16
FULL = jnp.float32
VMEM_LIMIT = 60 * 1024 * 1024


def dot_nt(a, b):
    return lax.dot_general(a, b, (((1,), (1,)), ((), ())), preferred_element_type=FULL)


def dot_nn(a, b):
    return lax.dot_general(a, b, (((1,), (0,)), ((), ())), preferred_element_type=FULL)


def dot_tn(a, b):
    return lax.dot_general(a, b, (((0,), (0,)), ((), ())), preferred_element_type=FULL)


def normalize(values):
    centre = jnp.mean(values, axis=-1, keepdims=True)
    shifted = values - centre
    spread = lax.rsqrt(jnp.mean(shifted * shifted, axis=-1, keepdims=True) + EPSILON)
    return (shifted * spread, spread)


def norm_back(d_hat, normal, spread):
    first = jnp.mean(d_hat, axis=-1, keepdims=True)
    second = jnp.mean(d_hat * normal, axis=-1, keepdims=True)
    return spread * (d_hat - first - normal * second)


def row_order(quarter, rl, heads):
    n = heads * quarter
    half = rl // 2
    out = lax.broadcasted_iota(jnp.int32, (n, n), 0)
    src = lax.broadcasted_iota(jnp.int32, (n, n), 1)
    h = lax.rem(out // half, heads)
    j = (out // (half * heads)) * half + lax.rem(out, half)
    return src == h * quarter + j


def main_kernel(
    len_ref, q_ref,
    x_ref, cot_ref, cots_ref, bias_ref,
    wkv_ref, wqg_ref, wot_ref, up_ref, down_ref, gain_ref,
    *rest,
    start, first, heads, width, rl, variants, depth,
):
    (
        res_ref, ress_ref, dmid_ref, near_ref, far_ref, dbk_ref, dbs_ref,
        gkv_ref, gqg_ref, gout_ref, gup_ref, gdown_ref, ggain_ref,
        n_s, kv_s, dkv_s, e_s, nq_s, q_s, o_s, r_s, g_s, dos_s, xn_s, hid_s, dpre_s, sh_s, dml_s, gated_s, dqg_s,
        bias_s, dbias_s, dn_s, cot_s, out_s,
    ) = rest[-35:]
    grad_refs = (gkv_ref, gqg_ref, gout_ref, gup_ref, gdown_ref, ggain_ref)
    item = pl.program_id(0)
    blk = pl.program_id(1)
    length = len_ref[start + item]
    y = q_ref[0] // 2
    core = lax.rem(q_ref[0], 2)
    _, ib, res, c = x_ref.shape
    quarter = cot_ref.shape[2]
    half = 2 * quarter
    tokens = ib * half
    hj = heads * quarter
    part = rl // 2
    groups = quarter // rl
    score = 1.0 / math.sqrt(width)

    lane_head = lax.broadcasted_iota(jnp.int32, (1, c), 1) // width
    head_masks = [(lane_head == h).astype(FULL) for h in range(heads)]

    def block_diag(v):
        v = v.astype(FULL)
        if part % 16 == 0:
            return jnp.concatenate(
                [(v[g * part : (g + 1) * part] * m).astype(LOW) for g in range(2 * groups) for m in head_masks], axis=0
            )
        rows = jnp.concatenate([v * m for m in head_masks], axis=0).astype(LOW)
        return dot_nn(row_order(quarter, rl, heads).astype(LOW), rows).astype(LOW)

    def pick(t):
        if part % 16:
            order = row_order(quarter, rl, heads).astype(FULL)
            t = lax.dot_general(
                order, t, (((0,), (0,)), ((), ())), precision=lax.Precision.HIGHEST, preferred_element_type=FULL
            )
            size, count = quarter, 1
        else:
            size, count = part, 2 * groups
        parts = []
        for g in range(count):
            base = g * heads * size
            r = t[base + (heads - 1) * size : base + heads * size]
            for h in range(heads - 2, -1, -1):
                r = jnp.where(lane_head == h, t[base + h * size : base + (h + 1) * size], r)
            parts.append(r)
        return jnp.concatenate(parts, axis=0)

    @pl.when(jnp.logical_and(item == 0, blk == 0))
    def _():
        for n, ref in enumerate(grad_refs):
            ref[...] = jnp.zeros_like(ref) if first else rest[n][...]

    @pl.when(blk == 0)
    def _():
        real = lax.broadcasted_iota(jnp.int32, (res, hj), 0) < length
        for jq in range(2):
            b = jnp.concatenate([bias_ref[0, jq, g] for g in range(groups)], axis=1).astype(FULL) * LOG2E
            bias_s[jq] = jnp.where(real, b, -1e9)
        dbias_s[...] = jnp.zeros_like(dbias_s)

    def at(index, size):
        return pl.ds(pl.multiple_of(index * size, size), size)

    g0 = gain_ref[0:1, :]
    g1 = gain_ref[1:2, :]
    g2 = gain_ref[2:3, :]
    g3 = gain_ref[3:4, :]

    def forward(kx):
        cot_s[:, at(core, quarter), :] = cot_ref[0]
        cot_s[:, at(1 - core, quarter), :] = cots_ref[0]
        xq = x_ref[0, :, at(y, half), :].reshape(tokens, c).astype(FULL)
        nq = (normalize(xq)[0] * g0 + g1).astype(LOW)
        nq_s[...] = nq
        qg = dot_nn(nq, wqg_ref[...]).astype(LOW).astype(FULL)
        q_s[...] = (qg[:, :c] * (score * LOG2E)).astype(LOW)
        g_s[...] = jax.nn.sigmoid(qg[:, c:])

        x = x_ref[0, :, :kx, :].reshape(ib * kx, c).astype(FULL)
        n = (normalize(x)[0] * g0 + g1).astype(LOW)
        n_s[: ib * kx] = n
        kv_s[: ib * kx] = dot_nn(n, wkv_ref[...]).astype(LOW)
        ones = jnp.ones((kx, c), LOW)
        units = [(i, jq) for i in range(ib) for jq in range(2)]

        def scores(i, jq):
            row = i * half + jq * quarter
            qbd = block_diag(q_s[row : row + quarter])
            return dot_nt(kv_s[i * kx : (i + 1) * kx, :c], qbd) + bias_s[jq, :kx, :]

        ahead = [scores(*u) for u in units[:depth]]
        for t, (i, jq) in enumerate(units):
            s = ahead.pop(0)
            if t + depth < len(units):
                ahead.append(scores(*units[t + depth]))
            eb = jnp.exp2(s - jnp.max(s, axis=0, keepdims=True)).astype(LOW)
            e_s[i * kx : (i + 1) * kx, jq * hj : (jq + 1) * hj] = eb
            v = kv_s[i * kx : (i + 1) * kx, c:]
            rows = slice(i * half + jq * quarter, i * half + (jq + 1) * quarter)
            o = dot_tn(eb, jnp.concatenate([v, ones], axis=1))
            o_s[rows, :] = pick(o[:, :c])
            r_s[rows, :] = 1.0 / pick(o[:, c:])

    def middle():
        rinv = r_s[...]
        blended = o_s[...] * rinv
        gate = g_s[...]
        gated = (gate * blended).astype(LOW)
        gated_s[...] = gated
        mid = x_ref[0, :, at(y, half), :].reshape(tokens, c).astype(FULL) + dot_nt(gated, wot_ref[...])
        n2, spread = normalize(mid)
        shaped = (n2 * g2 + g3).astype(LOW)
        sh_s[...] = shaped
        hp = dot_nn(shaped, up_ref[...])
        sg = 0.5 * jnp.tanh(0.5 * hp) + 0.5
        silu = hp * sg
        hid = silu.astype(LOW)
        hid_s[...] = hid
        out_s[...] = (mid + dot_nn(hid, down_ref[...])).astype(LOW).reshape(ib, half, c)
        cot = cot_s[...].reshape(tokens, c)
        dh = dot_nt(cot, down_ref[...])
        dpre = (dh * (sg + silu * (1.0 - sg))).astype(LOW)
        dpre_s[...] = dpre
        dsh = dot_nt(dpre, up_ref[...])
        ggain_ref[2:3, :] += jnp.sum(dsh * n2, axis=0, keepdims=True)
        ggain_ref[3:4, :] += jnp.sum(dsh, axis=0, keepdims=True)
        dmid = cot.astype(FULL) + norm_back(dsh * g2, n2, spread)
        dml = dmid.astype(LOW)
        dml_s[...] = dml
        dmid_ref[0] = dml.reshape(ib, half, c)
        dgated = dot_nn(dml, wot_ref[...])
        dblend = dgated * gate
        dqg_s[:, c:] = (dblend * blended * (1.0 - gate)).astype(LOW)
        dos = (dblend * rinv).astype(LOW)
        dos_s[...] = dos
        xn_s[...] = (-dos.astype(FULL) * blended).astype(LOW)
        gdown_ref[...] += dot_tn(cot, hid_s[...])
        gup_ref[...] += dot_tn(sh_s[...], dpre_s[...])
        gout_ref[...] += dot_tn(dml_s[...], gated_s[...])
        res_ref[0] = out_s[:, at(core, quarter), :]
        ress_ref[0] = out_s[:, at(1 - core, quarter), :]

    def backward(kx):
        ones = jnp.ones((kx, c), LOW)
        units = [(i, jq) for i in range(ib) for jq in range(2)]

        def d_scores(i, jq):
            row = i * half + jq * quarter
            dbd = block_diag(dos_s[row : row + quarter])
            xbd = block_diag(xn_s[row : row + quarter])
            v_one = jnp.concatenate([kv_s[i * kx : (i + 1) * kx, c:], ones], axis=1)
            return dot_nt(v_one, jnp.concatenate([dbd, xbd], axis=1)), dbd

        ahead = [d_scores(*u) for u in units[:depth]]
        for t, (i, jq) in enumerate(units):
            dp, dbd = ahead.pop(0)
            if t + depth < len(units):
                ahead.append(d_scores(*units[t + depth]))
            span = slice(i * kx, (i + 1) * kx)
            rows = slice(i * half + jq * quarter, i * half + (jq + 1) * quarter)
            eb = e_s[span, jq * hj : (jq + 1) * hj]
            dl = eb.astype(FULL) * dp
            dbias_s[jq, :kx, :] += dl
            dlb = dl.astype(LOW)
            qbd = block_diag(q_s[rows])
            dqg_s[rows, :c] = (pick(dot_tn(dlb, kv_s[span, :c])) * score).astype(LOW)
            if jq == 0:
                held = (dbd, qbd, dlb)
            else:
                dbd = jnp.concatenate([held[0], dbd], axis=0)
                qbd = jnp.concatenate([held[1], qbd], axis=0)
                dlb = jnp.concatenate([held[2], dlb], axis=1)
                dkv_s[span, c:] = dot_nn(e_s[span, :], dbd).astype(LOW)
                dkv_s[span, :c] = (dot_nn(dlb, qbd) * LN2).astype(LOW)
        dkv = dkv_s[: ib * kx]
        gkv_ref[...] += dot_tn(n_s[: ib * kx], dkv)
        dn_s[:, :kx, :] = dot_nt(dkv, wkv_ref[...]).reshape(ib, kx, c)
        if kx < res:
            dn_s[:, kx:, :] = jnp.zeros((ib, res - kx, c), FULL)
        gqg_ref[...] += dot_tn(nq_s[...], dqg_s[...])
        dn_s[:, at(y, half), :] += dot_nt(dqg_s[...], wqg_ref[...]).reshape(ib, half, c)
        near_ref[0] = dn_s[:, at(y, half), :].astype(LOW)
        far_ref[0] = dn_s[:, at(1 - y, half), :].astype(LOW)

    def step(kx):
        forward(kx)
        middle()
        backward(kx)

    for index, kx in enumerate(variants):
        below = variants[index - 1] if index else 0
        pl.when(jnp.logical_and(length > below, length <= kx))(functools.partial(step, kx))

    @pl.when(blk == pl.num_programs(1) - 1)
    def _():
        lanes = heads * part
        for cc in range(2):
            pieces = []
            for jq in range(2):
                for g in range(groups):
                    for yy in range(2):
                        off = (g * 2 + cc) * lanes
                        t = dbias_s[jq, yy * half : (yy + 1) * half, off : off + lanes]
                        pieces.append(jnp.concatenate([t[:quarter], t[quarter:]], axis=1).astype(LOW))

            @pl.when(core == cc)
            def _():
                for n, t in enumerate(pieces):
                    dbk_ref[n, 0] = t

            @pl.when(core != cc)
            def _():
                for n, t in enumerate(pieces):
                    dbs_ref[n, 0] = t


def main_call(
    start, count, lengths, qidx, pair_rep, cot, cots, bias, weights, grads, result=None, after=(),
    *, ib=8, variants=(128, 192, 256), depth=4,
):
    items, rl, res, c = pair_rep.shape
    quarter = cot.shape[2]
    half = 2 * quarter
    hid = weights[3].shape[1]
    heads = 4
    width = c // heads
    rows = rl // 2
    ib = min(ib, rows)
    tokens = ib * half
    hj = heads * quarter
    steps = rows // ib
    groups = quarter // rl
    n_rows = res // rl
    grad_shapes = [(c, 2 * c), (c, 2 * c), (c, c), (c, hid), (c, hid), (8, c)]

    def whole(shape):
        return pl.BlockSpec(shape, lambda b, i, *_: (0,) * len(shape))

    def own_rows(b, i, ln, q):
        return (start + b, lax.rem(q[0], 2) * steps + i, 0, 0)

    def chunk(size):
        return pl.BlockSpec((1, ib, size, c), lambda b, i, ln, q: (b, i, 0, 0))

    any_spec = pl.BlockSpec(memory_space=pl.ANY)
    cot_spec = pl.BlockSpec((1, ib, quarter, c), own_rows)
    db_spec = pl.BlockSpec((n_rows, 1, quarter, heads * rl), lambda b, i, ln, q: (0, b, 0, 0))
    first = result is None
    extra = () if first else (*grads, result)
    extra_specs = [] if first else [whole(s) for s in grad_shapes] + [any_spec]
    return pl.pallas_call(
        functools.partial(
            main_kernel, start=start, first=first, heads=heads, width=width, rl=rl, variants=variants, depth=depth
        ),
        grid_spec=pltpu.PrefetchScalarGridSpec(
            num_scalar_prefetch=2,
            grid=(count, steps),
            in_specs=[
                pl.BlockSpec((1, ib, res, c), own_rows),
                cot_spec,
                pl.BlockSpec((1, ib, quarter, c), lambda b, i, ln, q: (start + b, i, 0, 0)),
                pl.BlockSpec((1,) + bias.shape[1:], lambda b, i, ln, q: (start + b, 0, 0, 0, 0)),
            ]
            + [whole(w.shape) for w in weights]
            + extra_specs
            + [any_spec] * len(after),
            out_specs=[cot_spec, chunk(quarter), chunk(half), chunk(half), chunk(half), db_spec, db_spec]
            + [whole(s) for s in grad_shapes],
            scratch_shapes=[
                pltpu.VMEM((ib * res, c), LOW),
                pltpu.VMEM((ib * res, 2 * c), LOW),
                pltpu.VMEM((ib * res, 2 * c), LOW),
                pltpu.VMEM((ib * res, 2 * hj), LOW),
                pltpu.VMEM((tokens, c), LOW),
                pltpu.VMEM((tokens, c), LOW),
                pltpu.VMEM((tokens, c), FULL),
                pltpu.VMEM((tokens, c), FULL),
                pltpu.VMEM((tokens, c), FULL),
                pltpu.VMEM((tokens, c), LOW),
                pltpu.VMEM((tokens, c), LOW),
                pltpu.VMEM((tokens, hid), LOW),
                pltpu.VMEM((tokens, hid), LOW),
                pltpu.VMEM((tokens, c), LOW),
                pltpu.VMEM((tokens, c), LOW),
                pltpu.VMEM((tokens, c), LOW),
                pltpu.VMEM((tokens, 2 * c), LOW),
                pltpu.VMEM((2, res, hj), FULL),
                pltpu.VMEM((2, res, hj), FULL),
                pltpu.VMEM((ib, res, c), FULL),
                pltpu.VMEM((ib, half, c), LOW),
                pltpu.VMEM((ib, half, c), LOW),
            ],
        ),
        out_shape=[
            jax.ShapeDtypeStruct((items, rl, quarter, c), LOW),
            jax.ShapeDtypeStruct((count, rows, quarter, c), LOW),
            jax.ShapeDtypeStruct((count, rows, half, c), LOW),
            jax.ShapeDtypeStruct((count, rows, half, c), LOW),
            jax.ShapeDtypeStruct((count, rows, half, c), LOW),
            jax.ShapeDtypeStruct((n_rows, count, quarter, heads * rl), LOW),
            jax.ShapeDtypeStruct((n_rows, count, quarter, heads * rl), LOW),
        ]
        + [jax.ShapeDtypeStruct(s, FULL) for s in grad_shapes],
        input_output_aliases={} if first else {18: 0},
        compiler_params=pltpu.CompilerParams(
            dimension_semantics=("arbitrary", "arbitrary"), vmem_limit_bytes=VMEM_LIMIT
        ),
        cost_estimate=pl.CostEstimate(
            flops=800_000_000 * count * rl, bytes_accessed=300_000 * count * rl, transcendentals=0
        ),
        name="layer",
    )(lengths, qidx, pair_rep, cot, cots, bias, *weights, *extra, *after)


MESH = pl.DeviceIdType.MESH
MOMENTUM = 0.9
AVERAGE = 0.6
RATES = (0.5, 0.3, 3.0, 0.05, 0.03, 0.1)
CHUNKS = (5, 4, 3)


def pad16(n):
    return -(-n // 16) * 16


def greet_all(n_dev, n_heads, me):
    barrier = pltpu.get_barrier_semaphore()

    def signal(s, _):
        d = lax.rem(me + s, n_dev)
        pl.semaphore_signal(barrier, inc=1, device_id=(d // n_heads, lax.rem(d, n_heads)), device_id_type=MESH)
        return 0

    lax.fori_loop(1, n_dev, signal, 0)
    pl.semaphore_wait(barrier, n_dev - 1)


def prep_kernel(
    x_hbm, cot_hbm, proj_ref, bw_ref, out_ref, up_ref, down_ref, gains_ref,
    wkv_ref, wqg_ref, wot_ref, upall_ref, downall_ref, gainall_ref, base_ref, bias_hbm, cots_hbm,
    stage, wbuf, proj_s, up_s, down_s, wot_s, base_s, stack_ref, xbuf, xhat, pbuf, cbuf,
    x_sem, wsend, wrecv, bsend, brecv, self_sem, fsend, frecv, c_sem,
    *, n_rows, n_heads, parts,
):
    items, rl, res, c = x_hbm.shape
    hid = up_ref.shape[1]
    quarter = res // n_heads
    width = out_ref.shape[0]
    n_dev = n_rows * n_heads
    group = n_rows // n_heads
    lanes = n_heads * rl
    r = lax.axis_index("rows")
    q = lax.axis_index("heads")
    me = r * n_heads + q

    def load(b):
        span = pl.ds(pl.multiple_of(q * quarter, quarter), quarter)
        return pltpu.make_async_copy(x_hbm.at[b, :, span, :], xbuf.at[b], x_sem.at[b])

    rows = rl // 2
    other = pl.ds(pl.multiple_of((1 - lax.rem(q, 2)) * rows, rows), rows)
    cot_in = pltpu.make_async_copy(cot_hbm.at[:, other, :, :], cbuf, c_sem.at[0])
    cot_out = pltpu.make_async_remote_copy(
        src_ref=cbuf,
        dst_ref=cots_hbm,
        send_sem=c_sem.at[1],
        recv_sem=c_sem.at[2],
        device_id=(r, q + 1 - 2 * lax.rem(q, 2)),
        device_id_type=MESH,
    )
    for b in range(items):
        load(b).start()
    cot_in.start()

    pr, ur, dr, cr, cd = c // n_rows, c // n_dev, hid // n_dev, c // n_rows, c // n_dev
    o_down = pad16(pr)
    o_up = o_down + pad16(dr)
    o_out = o_up + pad16(ur * (hid // c))
    o_misc = o_out + pad16(cr)
    lane = lax.broadcasted_iota(jnp.int32, (1, c), 1)
    stage[...] = jnp.zeros_like(stage)
    stage[:pr, :] = proj_ref[...]
    stage[o_down : o_down + dr, :] = down_ref[...]
    for g in range(hid // c):
        stage[o_up + g * ur : o_up + (g + 1) * ur, :] = up_ref[:, g * c : (g + 1) * c]
    spot = lax.broadcasted_iota(jnp.int32, (width, c), 1) == q * width + lax.broadcasted_iota(jnp.int32, (width, c), 0)
    stage[o_out : o_out + cr, :] = dot_tn(out_ref[...].astype(LOW), spot.astype(LOW))
    stage[o_misc : o_misc + pr, 0:1] = bw_ref[...]
    stage[o_misc : o_misc + 4, c // 2 : c // 2 + cd] = gains_ref[...]
    wbuf[me] = stage[...].astype(LOW)

    greet_all(n_dev, n_heads, me)

    def weights_to(s):
        d = lax.rem(me + s, n_dev)
        return pltpu.make_async_remote_copy(
            src_ref=wbuf.at[me],
            dst_ref=wbuf.at[me],
            send_sem=wsend.at[s],
            recv_sem=wrecv.at[s],
            device_id=(d // n_heads, lax.rem(d, n_heads)),
            device_id_type=MESH,
        )

    def start_one(s, _):
        weights_to(s).start()
        return 0

    lax.fori_loop(1, n_dev, start_one, 0)

    for b in range(items):
        load(b).wait()
        xhat[b] = normalize(xbuf[b].reshape(rl * quarter, c).astype(FULL))[0]

    cot_in.wait()
    cot_out.start()

    def wait_one(s, _):
        weights_to(s).wait()
        return 0

    lax.fori_loop(1, n_dev, wait_one, 0)

    head_of = lax.rem(lane // (rl // 2), n_heads)
    gain_sum = jnp.zeros((16, c), FULL)
    for rr in range(n_rows):
        wot = jnp.zeros((cr, c), FULL)
        base = jnp.zeros((pr, c), FULL)
        for h in range(n_heads):
            d = rr * n_heads + h
            proj_s[rr * pr : (rr + 1) * pr, h * c : (h + 1) * c] = wbuf[d, :pr].astype(FULL)
            wot = wot + wbuf[d, o_out : o_out + cr].astype(FULL)
            misc = wbuf[d, o_misc : o_misc + 16].astype(FULL)
            base = base + jnp.where(head_of == h, misc[:pr, 0:1], 0.0)
            moved = pltpu.roll(misc, (d * cd + c // 2) % c, 1)
            gain_sum = gain_sum + jnp.where(lane // cd == d, moved, 0.0)
            down_s[d * dr : (d + 1) * dr, :] = wbuf[d, o_down : o_down + dr].astype(FULL)
            for g in range(hid // c):
                rows = slice(o_up + g * ur, o_up + (g + 1) * ur)
                up_s[d * ur : (d + 1) * ur, g * c : (g + 1) * c] = wbuf[d, rows].astype(FULL)
        wot_s[rr * cr : (rr + 1) * cr, :] = wot
        base_s[rr * pr : (rr + 1) * pr, :] = base
    wot_ref[...] = wot_s[...].astype(LOW)
    downall_ref[...] = down_s[...].astype(LOW)
    upall_ref[...] = up_s[...].astype(LOW)
    gainall_ref[...] = gain_sum[:8]
    src = lax.broadcasted_iota(jnp.int32, (n_heads * c, 2 * c), 0)
    dst = lax.broadcasted_iota(jnp.int32, (n_heads * c, 2 * c), 1)
    place = (lax.rem(dst, c) // width) * c + lax.rem(dst, width)
    second = dst // c
    proj_low = proj_s[...].astype(LOW)
    wqg_ref[...] = dot_nn(proj_low, (src == place + second * 3 * width).astype(LOW)).astype(LOW)
    wkv_ref[...] = dot_nn(proj_low, (src == place + width + second * width).astype(LOW)).astype(LOW)
    base = base_s[...]
    row_of = (lane // (rl // 2 * n_heads)) * (rl // 2) + lax.rem(lane, rl // 2)
    base_ref[...] = base[:, :lanes].astype(LOW)
    for jj in range(rl):
        stack_ref[jj * c : (jj + 1) * c, :] = jnp.where(row_of == jj, base, 0.0)[:, :lanes].astype(LOW)

    g0 = gain_sum[0:1]
    g1 = gain_sum[1:2]
    target = r // group
    core = lax.rem(q, 2)
    slot = lax.rem(r, group)
    span = pl.ds(pl.multiple_of(q * quarter, quarter), quarter)
    size = items // parts

    def own_copy(p):
        return pltpu.make_async_copy(
            pbuf.at[pl.ds(p * size, size)], bias_hbm.at[pl.ds(p * size, size), core, slot, span, :], self_sem.at[p]
        )

    def bias_to(p, t, s):
        return pltpu.make_async_remote_copy(
            src_ref=pbuf.at[pl.ds(p * size, size)],
            dst_ref=bias_hbm.at[pl.ds(p * size, size), lax.rem(target, 2), slot, span, :],
            send_sem=bsend.at[p, t],
            recv_sem=brecv.at[p, s],
            device_id=(t, target),
            device_id_type=MESH,
        )

    mine = slot * n_heads + q
    for p in range(parts):

        def piece(b, _):
            n = (xhat[b] * g0 + g1).astype(LOW).reshape(rl, quarter, c)
            wide = jnp.concatenate([n[jj] for jj in range(rl)], axis=1)
            pbuf[b] = dot_nn(wide, stack_ref[...]).astype(LOW)
            return 0

        lax.fori_loop(p * size, (p + 1) * size, piece, 0)

        def send(t, _):
            is_me = jnp.logical_and(t == r, target == q)

            @pl.when(is_me)
            def _():
                own_copy(p).start()

            @pl.when(jnp.logical_not(is_me))
            def _():
                bias_to(p, t, mine).start()

            return 0

        lax.fori_loop(0, n_rows, send, 0)

    def forward(p):
        ref = bias_hbm.at[pl.ds(p * size, size), core]
        return pltpu.make_async_remote_copy(
            src_ref=ref,
            dst_ref=ref,
            send_sem=fsend.at[p],
            recv_sem=frecv.at[p],
            device_id=(r, q + 1 - 2 * core),
            device_id_type=MESH,
        )

    for p in range(parts):

        def finish(t, _):
            is_me = jnp.logical_and(t == r, target == q)

            @pl.when(is_me)
            def _():
                own_copy(p).wait()

            @pl.when(jnp.logical_not(is_me))
            def _():
                bias_to(p, t, mine).wait_send()

            from_me = jnp.logical_and(q * group + t // n_heads == r, lax.rem(t, n_heads) == q)

            @pl.when(jnp.logical_not(from_me))
            def _():
                bias_to(p, t, t).wait_recv()

            return 0

        lax.fori_loop(0, n_rows, finish, 0)
        forward(p).start()

    for p in range(parts):
        forward(p).wait()
    cot_out.wait()


def prep_call(pair_rep, cot, weights, n_rows, n_heads, quarter, parts=3):
    items, rl, res, c = pair_rep.shape
    proj, bw, out, up, down, gains = weights
    hid = up.shape[1]
    n_dev = n_rows * n_heads
    group = n_rows // n_heads
    lanes = n_heads * rl
    width = out.shape[0]
    rows = 2 * pad16(c // n_rows) + pad16(hid // n_dev) + pad16(c // n_dev * (hid // c)) + 16
    vmem = pl.BlockSpec(memory_space=pltpu.VMEM)
    hbm = pl.BlockSpec(memory_space=pl.ANY)
    return pl.pallas_call(
        functools.partial(prep_kernel, n_rows=n_rows, n_heads=n_heads, parts=parts),
        in_specs=[hbm, hbm] + [vmem] * 6,
        out_specs=[vmem] * 7 + [hbm, hbm],
        out_shape=[
            jax.ShapeDtypeStruct((c, 2 * c), LOW),
            jax.ShapeDtypeStruct((c, 2 * c), LOW),
            jax.ShapeDtypeStruct((c, c), LOW),
            jax.ShapeDtypeStruct((c, hid), LOW),
            jax.ShapeDtypeStruct((hid, c), LOW),
            jax.ShapeDtypeStruct((8, c), FULL),
            jax.ShapeDtypeStruct((c, lanes), LOW),
            jax.ShapeDtypeStruct((items, 2, group, res, lanes), LOW),
            jax.ShapeDtypeStruct((items, rl // 2, quarter, c), LOW),
        ],
        scratch_shapes=[
            pltpu.VMEM((rows, c), FULL),
            pltpu.VMEM((n_dev, rows, c), LOW),
            pltpu.VMEM((c, n_heads * c), FULL),
            pltpu.VMEM((c, hid), FULL),
            pltpu.VMEM((hid, c), FULL),
            pltpu.VMEM((c, c), FULL),
            pltpu.VMEM((c, c), FULL),
            pltpu.VMEM((rl * c, lanes), LOW),
            pltpu.VMEM((items, rl, quarter, c), LOW),
            pltpu.VMEM((items, rl * quarter, c), FULL),
            pltpu.VMEM((items, quarter, lanes), LOW),
            pltpu.VMEM((items, rl // 2, quarter, c), LOW),
            pltpu.SemaphoreType.DMA((items,)),
            pltpu.SemaphoreType.DMA((n_dev,)),
            pltpu.SemaphoreType.DMA((n_dev,)),
            pltpu.SemaphoreType.DMA((parts, n_rows)),
            pltpu.SemaphoreType.DMA((parts, n_rows)),
            pltpu.SemaphoreType.DMA((parts,)),
            pltpu.SemaphoreType.DMA((parts,)),
            pltpu.SemaphoreType.DMA((parts,)),
            pltpu.SemaphoreType.DMA((3,)),
        ],
        compiler_params=pltpu.CompilerParams(
            collective_id=0, has_side_effects=True, vmem_limit_bytes=VMEM_LIMIT
        ),
        name="prep",
    )(pair_rep, cot, *weights)


def finish_kernel(
    x_hbm, *refs, n_rows, n_heads, sizes,
):
    n = len(sizes)
    refs = list(refs)
    take = lambda k: [refs.pop(0) for _ in range(k)]
    dmid_hbm, near_hbm, far_hbm, dbk_refs = take(n), take(n), take(n), take(n)
    dbr_refs = take(n - 1)
    (dbs_hbm,) = take(1)
    gqg_ref, gkv_ref, gout_ref, gup_ref, gdown_ref, gtwo_ref, gain_ref, base_ref = take(8)
    pair_hbm, proj_ref, out_ref, up_ref, down_ref, small_ref = take(6)
    xb, mb, nb, fb, ob, sb, dsum, dbuf, dtmp, proj_s, down_s, stage, gsrc, gbuf, ggain_s, gbias_s, sbuf = take(17)
    in_sem, far_send, far_recv, pre_sem, dsend, drecv, dself, gsend, grecv, gself, out_sem, osend, orecv, ssend, srecv = refs

    items = sum(sizes)
    starts = [sum(sizes[:i]) for i in range(n)]
    last = n - 1
    n_dev = n_rows * n_heads
    c = gqg_ref.shape[0]
    hid = gup_ref.shape[1]
    width = c // n_heads
    group = n_rows // n_heads
    _, rows, half, _ = xb.shape
    quarter = half // 2
    tokens = rows * half
    lanes = base_ref.shape[1]
    r = lax.axis_index("rows")
    q = lax.axis_index("heads")
    me = r * n_heads + q
    y = q // 2
    core = lax.rem(q, 2)
    sibling = (r, q + 1 - 2 * core)
    across = (r, q + 2 - 4 * y)

    def at(index, size):
        return pl.ds(pl.multiple_of(index * size, size), size)

    loads = []
    for ch in range(n):
        for i in range(sizes[ch]):
            b = starts[ch] + i
            one = [
                pltpu.make_async_copy(x_hbm.at[b, at(core, rows), at(y, half), :], xb.at[b], in_sem.at[0, b]),
                pltpu.make_async_copy(dmid_hbm[ch].at[i], mb.at[b], in_sem.at[1, b]),
                pltpu.make_async_copy(near_hbm[ch].at[i], nb.at[b], in_sem.at[2, b]),
            ]
            if ch != last:
                one.append(pltpu.make_async_copy(far_hbm[ch].at[i], fb.at[b], in_sem.at[3, b]))
            loads += one
    for load in loads:
        load.start()

    greet_all(n_dev, n_heads, me)

    pre = pltpu.make_async_remote_copy(
        src_ref=dbs_hbm,
        dst_ref=dtmp,
        send_sem=pre_sem.at[0],
        recv_sem=pre_sem.at[1],
        device_id=sibling,
        device_id_type=MESH,
    )
    pre.start()

    def far_copy(i):
        return pltpu.make_async_remote_copy(
            src_ref=far_hbm[last].at[i],
            dst_ref=fb.at[starts[last] + i],
            send_sem=far_send.at[i],
            recv_sem=far_recv.at[i],
            device_id=across,
            device_id_type=MESH,
        )

    for i in range(sizes[last]):
        far_copy(i).start()

    def db_to(ch, t):
        span = pl.ds(starts[ch], sizes[ch])
        return pltpu.make_async_remote_copy(
            src_ref=dsum.at[t, span],
            dst_ref=dbuf.at[r, span],
            send_sem=dsend.at[ch, t],
            recv_sem=drecv.at[ch, r],
            device_id=(y * 2 * group + t // 2, lax.rem(t, 2) * 2 + core),
            device_id_type=MESH,
        )

    def db_from(ch, t):
        span = pl.ds(starts[ch], sizes[ch])
        return pltpu.make_async_remote_copy(
            src_ref=dsum.at[t, span],
            dst_ref=dbuf.at[t, span],
            send_sem=dsend.at[ch, t],
            recv_sem=drecv.at[ch, t],
            device_id=(t, q),
            device_id_type=MESH,
        )

    def db_own(ch, t):
        span = pl.ds(starts[ch], sizes[ch])
        return pltpu.make_async_copy(dsum.at[t, span], dbuf.at[r, span], dself.at[ch])

    def is_me(t):
        return jnp.logical_and(y * 2 * group + t // 2 == r, lax.rem(t, 2) == y)

    def from_me(t):
        return jnp.logical_and(t == r, r // (2 * group) == y)

    def db_send(ch):
        def start(t, _):
            @pl.when(is_me(t))
            def _():
                db_own(ch, t).start()

            @pl.when(jnp.logical_not(is_me(t)))
            def _():
                db_to(ch, t).start()

            return 0

        lax.fori_loop(0, n_rows, start, 0)

    def db_wait(ch):
        def wait(t, _):
            @pl.when(is_me(t))
            def _():
                db_own(ch, t).wait()

            @pl.when(jnp.logical_not(is_me(t)))
            def _():
                db_to(ch, t).wait_send()

            @pl.when(jnp.logical_not(from_me(t)))
            def _():
                db_from(ch, t).wait_recv()

            return 0

        lax.fori_loop(0, n_rows, wait, 0)

    for ch in range(last):
        span = slice(starts[ch], starts[ch] + sizes[ch])
        dsum[:, span] = (dbk_refs[ch][...].astype(FULL) + dbr_refs[ch][...].astype(FULL)).astype(LOW)
        db_send(ch)
    pre.wait()
    dsum[:, starts[last] :] = (dbk_refs[last][...].astype(FULL) + dtmp[...].astype(FULL)).astype(LOW)
    db_send(last)

    pr, ur, dr, cr = c // n_rows, c // n_dev, hid // n_dev, c // n_rows
    o_down = pad16(pr)
    o_up = o_down + pad16(dr)
    o_out = o_up + pad16(ur * (hid // c))
    wide = n_heads * c
    dst = lax.broadcasted_iota(jnp.int32, (wide, wide), 1)
    kind = lax.rem(dst, c) // width
    spot = jnp.where(kind == 0, 0, jnp.where(kind == 3, 1, kind + 1)) * c + (dst // c) * width + lax.rem(dst, width)
    perm = (lax.broadcasted_iota(jnp.int32, (wide, wide), 0) == spot).astype(LOW)
    mixed = jnp.concatenate([gqg_ref[...].astype(LOW), gkv_ref[...].astype(LOW)], axis=1)
    proj_s[...] = dot_nn(mixed, perm)
    down_s[...] = gdown_ref[...].T
    if pr % 16 or dr % 16 or (ur * (hid // c)) % 16:
        stage[...] = jnp.zeros_like(stage)
    for d in range(n_dev):
        rr, h = d // n_heads, d % n_heads
        stage[d, :pr, :] = proj_s[rr * pr : (rr + 1) * pr, h * c : (h + 1) * c]
        stage[d, o_down : o_down + dr, :] = down_s[d * dr : (d + 1) * dr, :]
        for g in range(hid // c):
            stage[d, o_up + g * ur : o_up + (g + 1) * ur, :] = gup_ref[d * ur : (d + 1) * ur, g * c : (g + 1) * c]
        stage[d, o_out : o_out + cr, :] = gout_ref[rr * cr : (rr + 1) * cr, :]
    gsrc[...] = stage[...].astype(LOW)

    def to_all(src, dst, sends, recvs, s):
        d = lax.rem(me + s, n_dev)
        return pltpu.make_async_remote_copy(
            src_ref=src.at[d] if src is gsrc else src.at[me],
            dst_ref=dst.at[me],
            send_sem=sends.at[s],
            recv_sem=recvs.at[s],
            device_id=(d // n_heads, lax.rem(d, n_heads)),
            device_id_type=MESH,
        )

    def start_all(*args):
        def start(s, _):
            to_all(*args, s).start()
            return 0

        lax.fori_loop(1, n_dev, start, 0)

    def wait_all(*args):
        def wait(s, _):
            to_all(*args, s).wait()
            return 0

        lax.fori_loop(1, n_dev, wait, 0)

    start_all(gsrc, gbuf, gsend, grecv)
    own = pltpu.make_async_copy(gsrc.at[me], gbuf.at[me], gself.at[0])
    own.start()

    ggain_s[...] = jnp.zeros_like(ggain_s)
    gbias_s[...] = jnp.zeros_like(gbias_s)
    g0 = gain_ref[0:1, :]
    g1 = gain_ref[1:2, :]
    lane = lax.broadcasted_iota(jnp.int32, (1, lanes), 1)
    place = lax.rem(lane, rows) * 2 + lane // (rows * n_heads)

    def pair_local(b):
        return pltpu.make_async_copy(ob.at[b], pair_hbm.at[b, at(core, rows), :, :], out_sem.at[b])

    def pair_remote(b):
        return pltpu.make_async_remote_copy(
            src_ref=sb.at[b],
            dst_ref=pair_hbm.at[b, at(core, rows), :, :],
            send_sem=osend.at[b],
            recv_sem=orecv.at[b],
            device_id=sibling,
            device_id_type=MESH,
        )

    def item(b):
        normal, spread = normalize(xb[b].reshape(tokens, c).astype(FULL))
        normed = (normal * g0 + g1).astype(LOW)
        db = dbuf[0, b].astype(FULL)
        for t in range(1, n_rows):
            db = db + dbuf[t, b].astype(FULL)
        db = db.astype(LOW)
        spread_db = jnp.concatenate([jnp.where(place == t, db, jnp.zeros_like(db)) for t in range(2 * rows)], axis=0)
        gbias_s[...] += dot_tn(normed, spread_db)
        total = nb[b].astype(FULL) + fb[b].astype(FULL)
        dn = total.reshape(tokens, c) + dot_nt(spread_db, base_ref[...])
        ggain_s[0:1, :] += jnp.sum(dn * normal, axis=0, keepdims=True)
        ggain_s[1:2, :] += jnp.sum(dn, axis=0, keepdims=True)
        back = norm_back(dn * g0, normal, spread)
        mb[b] = (mb[b].astype(FULL) + back.reshape(rows, half, c)).astype(LOW)
        ob[b] = mb[b, :, at(core, quarter), :]
        sb[b] = mb[b, :, at(1 - core, quarter), :]
        pair_local(b).start()
        pair_remote(b).start()

    for load in loads:
        load.wait()
    for ch in range(n):
        db_wait(ch)
        if ch == last:
            for i in range(sizes[last]):
                far_copy(i).wait()

        def one(i, _):
            item(starts[ch] + i)
            return 0

        lax.fori_loop(0, sizes[ch], one, 0)

    heads = lax.broadcasted_iota(jnp.int32, (8, lanes), 0) - 2
    sel = (lax.rem(lax.broadcasted_iota(jnp.int32, (8, lanes), 1) // rows, n_heads) == heads).astype(FULL)
    brows = lax.dot_general(
        sel, gbias_s[...], (((1,), (1,)), ((), ())), precision=lax.Precision.HIGHEST, preferred_element_type=FULL
    )
    row = lax.broadcasted_iota(jnp.int32, (8, c), 0)
    two = pltpu.roll(gtwo_ref[...], 4, 0)
    sbuf[me] = jnp.where(row < 2, ggain_s[...], jnp.where(row < 6, brows, two))
    start_all(sbuf, sbuf, ssend, srecv)

    own.wait()
    wait_all(gsrc, gbuf, gsend, grecv)
    total = lax.fori_loop(0, n_dev, lambda d, t: t + gbuf[d].astype(FULL), jnp.zeros(gbuf.shape[1:], FULL))
    proj_ref[...] = total[:pr]
    out_ref[...] = total[o_out : o_out + cr]
    down_ref[...] = total[o_down : o_down + dr]
    for g in range(hid // c):
        up_ref[:, g * c : (g + 1) * c] = total[o_up + g * ur : o_up + (g + 1) * ur]
    wait_all(sbuf, sbuf, ssend, srecv)
    small_ref[...] = lax.fori_loop(0, n_dev, lambda d, t: t + sbuf[d], jnp.zeros(small_ref.shape, FULL))

    def leave(b, _):
        pair_local(b).wait()
        pair_remote(b).wait()
        return 0

    lax.fori_loop(0, items, leave, 0)


def finish_call(pair_rep, dmids, nears, fars, dbks, dbrs, dbs, grads, gains, base, n_rows, n_heads):
    gkv, gqg, gout, gup, gdown, gtwo = grads
    items, rl, res, _ = pair_rep.shape
    c, hid = gup.shape
    n_dev = n_rows * n_heads
    sizes = tuple(t.shape[0] for t in dmids)
    n = len(sizes)
    _, rows, half, _ = dmids[0].shape
    _, count, quarter, lanes = dbs.shape
    pr, ur, dr, cr = c // n_rows, c // n_dev, hid // n_dev, c // n_rows
    grows = 2 * pad16(pr) + pad16(dr) + pad16(ur * (hid // c))
    vmem = pl.BlockSpec(memory_space=pltpu.VMEM)
    hbm = pl.BlockSpec(memory_space=pl.ANY)
    dma = pltpu.SemaphoreType.DMA
    return pl.pallas_call(
        functools.partial(finish_kernel, n_rows=n_rows, n_heads=n_heads, sizes=sizes),
        in_specs=[hbm] * (1 + 3 * n) + [vmem] * (2 * n - 1) + [hbm] + [vmem] * 8,
        out_specs=[hbm] + [vmem] * 5,
        out_shape=[
            jax.ShapeDtypeStruct((items, rl, quarter, c), LOW),
            jax.ShapeDtypeStruct((pr, c), FULL),
            jax.ShapeDtypeStruct((cr, c), FULL),
            jax.ShapeDtypeStruct((ur, hid), FULL),
            jax.ShapeDtypeStruct((dr, c), FULL),
            jax.ShapeDtypeStruct((8, c), FULL),
        ],
        scratch_shapes=[pltpu.VMEM((items, rows, half, c), LOW)] * 4
        + [pltpu.VMEM((items, rows, quarter, c), LOW)] * 2
        + [pltpu.VMEM((n_rows, items, quarter, lanes), LOW)] * 2
        + [
            pltpu.VMEM(dbs.shape, LOW),
            pltpu.VMEM((c, n_heads * c), FULL),
            pltpu.VMEM((hid, c), FULL),
            pltpu.VMEM((n_dev, grows, c), FULL),
            pltpu.VMEM((n_dev, grows, c), LOW),
            pltpu.VMEM((n_dev, grows, c), LOW),
            pltpu.VMEM((8, c), FULL),
            pltpu.VMEM((c, lanes), FULL),
            pltpu.VMEM((n_dev, 8, c), FULL),
            dma((4, items)),
            dma((count,)),
            dma((count,)),
            dma((2,)),
            dma((n, n_rows)),
            dma((n, n_rows)),
            dma((n,)),
            dma((n_dev,)),
            dma((n_dev,)),
            dma((1,)),
            dma((items,)),
            dma((items,)),
            dma((items,)),
            dma((n_dev,)),
            dma((n_dev,)),
        ],
        compiler_params=pltpu.CompilerParams(
            collective_id=1, has_side_effects=True, vmem_limit_bytes=VMEM_LIMIT
        ),
        name="finish",
    )(pair_rep, *dmids, *nears, *fars, *dbks, *dbrs, dbs, gqg, gkv, gout, gup, gdown, gtwo, gains, base)


def place_kernel(q_ref, *refs, sizes):
    n = len(sizes)
    parts = refs[2 : 2 + n]
    out, _, buf, in_sem, out_sem = refs[2 + n :]
    rows = buf.shape[1]
    other = pl.ds(pl.multiple_of((1 - lax.rem(q_ref[0], 2)) * rows, rows), rows)
    loads = []
    stores = []
    for i, size in enumerate(sizes):
        span = pl.ds(sum(sizes[:i]), size)
        loads.append(pltpu.make_async_copy(parts[i], buf.at[span], in_sem.at[i]))
        stores.append(pltpu.make_async_copy(buf.at[span], out.at[span, other, :, :], out_sem.at[i]))
    for load in loads:
        load.start()
    for load, store in zip(loads, stores):
        load.wait()
        store.start()
    for store in stores:
        store.wait()


def place_call(qidx, result, d_pair, results):
    sizes = tuple(t.shape[0] for t in results)
    hbm = pl.BlockSpec(memory_space=pl.ANY)
    dma = pltpu.SemaphoreType.DMA
    return pl.pallas_call(
        functools.partial(place_kernel, sizes=sizes),
        in_specs=[pl.BlockSpec(memory_space=pltpu.SMEM)] + [hbm] * (2 + len(sizes)),
        out_specs=[hbm, hbm],
        out_shape=[jax.ShapeDtypeStruct(result.shape, LOW)] * 2,
        scratch_shapes=[
            pltpu.VMEM((sum(sizes),) + results[0].shape[1:], LOW),
            dma((len(sizes),)),
            dma((len(sizes),)),
        ],
        input_output_aliases={1: 0, 2: 1},
        compiler_params=pltpu.CompilerParams(vmem_limit_bytes=VMEM_LIMIT),
        name="place",
    )(qidx, result, d_pair, *results)


def update(weight, gradient, moment, average, step_rate, root_pairs):
    moment_next = MOMENTUM * moment + gradient
    weight_next = weight - step_rate / root_pairs * (gradient + MOMENTUM * moment_next)
    return (weight_next, moment_next, AVERAGE * average + (1.0 - AVERAGE) * weight_next)


def shards(
    pair_rep, lengths,
    proj_weight, bias_weight, out_weight, up_weight, down_weight, norm_gains,
    proj_moment, bias_moment, out_moment, up_moment, down_moment, gains_moment,
    proj_average, bias_average, out_average, up_average, down_average, gains_average,
    cotangent,
    *, n_rows, n_heads,
):
    both = ("rows", "heads")
    items, rl, res, c = pair_rep.shape
    quarter = cotangent.shape[2]
    hid = up_weight.shape[1]
    width = out_weight.shape[0]
    n_dev = n_rows * n_heads
    q = lax.axis_index("heads").astype(jnp.int32)
    r = lax.axis_index("rows").astype(jnp.int32)
    qidx = q.reshape(1)
    weights = (proj_weight, bias_weight, out_weight, up_weight, down_weight, norm_gains)
    sibling = [(d, d ^ 1) for d in range(n_dev)]
    across = [(d, d ^ 2) for d in range(n_dev)]
    wkv, wqg, wot, up, down, gains, base, bias, cots = prep_call(
        pair_rep, cotangent, weights, n_rows, n_heads, quarter
    )

    grads = ()
    result = None
    results, dmids, nears, fars, dbks, dbrs = [], [], [], [], [], []
    held = ()
    start = 0
    for n, count in enumerate(CHUNKS):
        outs = main_call(
            start, count, lengths, qidx, pair_rep, cotangent, cots, bias, (wkv, wqg, wot, up, down, gains), grads,
            result, held,
        )
        result, shared, dmid, near, far, dbk, dbs = outs[:7]
        grads = outs[7:]
        results.append(lax.ppermute(shared, both, sibling))
        held = (fars[-1], dbrs[-1]) if n else ()
        if n < len(CHUNKS) - 1:
            far = lax.ppermute(far, both, across)
            dbrs.append(lax.ppermute(dbs, both, sibling))
        dmids.append(dmid)
        nears.append(near)
        fars.append(far)
        dbks.append(dbk)
        start += count

    d_pair, s_proj, s_out, s_up, s_down, small = finish_call(
        pair_rep, dmids, nears, fars, dbks, dbrs, dbs, grads, gains, base, n_rows, n_heads
    )
    result, d_pair = place_call(qidx, result, d_pair, results)
    cd, cr = c // n_dev, c // n_rows
    own = lax.dynamic_slice(small, (0, (r * n_heads + q) * cd), (8, cd))
    s_gains = jnp.concatenate([own[:2], own[6:8]])
    s_bias = lax.dynamic_slice(small, (2 + q, r * cr), (1, cr)).reshape(cr, 1)
    s_out = lax.dynamic_slice(s_out, (0, q * width), (cr, width)).T
    sums = (s_proj, s_bias, s_out, s_up, s_down, s_gains)
    moments = (proj_moment, bias_moment, out_moment, up_moment, down_moment, gains_moment)
    averages = (proj_average, bias_average, out_average, up_average, down_average, gains_average)
    root_pairs = math.sqrt(items * res * res)
    nexts = [
        update(w, g.reshape(w.shape), m, a, rate, root_pairs)
        for w, g, m, a, rate in zip(weights, sums, moments, averages, RATES)
    ]
    return (
        result,
        d_pair,
        *[n[0] for n in nexts],
        *[n[1] for n in nexts],
        *[n[2] for n in nexts],
    )


def solution(mesh):
    weight_specs = (
        P("rows", "heads"),
        P("rows", "heads"),
        P("heads", "rows"),
        P(("rows", "heads"), None),
        P(("rows", "heads"), None),
        P(None, ("rows", "heads")),
    )
    quarter_spec = P(None, "rows", "heads", None)
    in_specs = (P(None, "rows", None, None), P()) + weight_specs * 3 + (quarter_spec,)
    out_specs = (quarter_spec, quarter_spec) + weight_specs * 3
    body = functools.partial(shards, n_rows=mesh.shape["rows"], n_heads=mesh.shape["heads"])
    return jax.shard_map(body, mesh=mesh, in_specs=in_specs, out_specs=out_specs, check_vma=False)
```

```python
import math
import functools
import jax
import jax.numpy as jnp
from jax import lax
from jax.experimental import pallas as pl
from jax.experimental.pallas import tpu as pltpu
from jax.sharding import PartitionSpec as P

EPSILON = 1e-05
LOG2E = 1.4426950408889634
LN2 = 0.6931471805599453
LOW = jnp.bfloat16
FULL = jnp.float32
VMEM_LIMIT = 60 * 1024 * 1024


def dot_nt(a, b):
    return lax.dot_general(a, b, (((1,), (1,)), ((), ())), preferred_element_type=FULL)


def dot_nn(a, b):
    return lax.dot_general(a, b, (((1,), (0,)), ((), ())), preferred_element_type=FULL)


def dot_tn(a, b):
    return lax.dot_general(a, b, (((0,), (0,)), ((), ())), preferred_element_type=FULL)


def normalize(values):
    centre = jnp.mean(values, axis=-1, keepdims=True)
    shifted = values - centre
    spread = lax.rsqrt(jnp.mean(shifted * shifted, axis=-1, keepdims=True) + EPSILON)
    return (shifted * spread, spread)


def norm_back(d_hat, normal, spread):
    first = jnp.mean(d_hat, axis=-1, keepdims=True)
    second = jnp.mean(d_hat * normal, axis=-1, keepdims=True)
    return spread * (d_hat - first - normal * second)


def row_order(quarter, rl, heads):
    n = heads * quarter
    half = rl // 2
    out = lax.broadcasted_iota(jnp.int32, (n, n), 0)
    src = lax.broadcasted_iota(jnp.int32, (n, n), 1)
    h = lax.rem(out // half, heads)
    j = (out // (half * heads)) * half + lax.rem(out, half)
    return src == h * quarter + j


def main_kernel(
    len_ref, q_ref,
    x_ref, cot_ref, cots_ref, bias_ref,
    wkv_ref, wqg_ref, wot_ref, up_ref, down_ref, gain_ref,
    *rest,
    start, first, heads, width, rl, variants, depth,
):
    (
        res_ref, ress_ref, dmid_ref, near_ref, far_ref, dbk_ref, dbs_ref,
        gkv_ref, gqg_ref, gout_ref, gup_ref, gdown_ref, ggain_ref,
        n_s, kv_s, dkv_s, e_s, nq_s, q_s, o_s, r_s, g_s, dos_s, xn_s, hid_s, dpre_s, sh_s, dml_s, gated_s, dqg_s,
        bias_s, dbias_s, dn_s, cot_s, out_s,
    ) = rest[-35:]
    grad_refs = (gkv_ref, gqg_ref, gout_ref, gup_ref, gdown_ref, ggain_ref)
    item = pl.program_id(0)
    blk = pl.program_id(1)
    length = len_ref[start + item]
    y = q_ref[0] // 2
    core = lax.rem(q_ref[0], 2)
    _, ib, res, c = x_ref.shape
    quarter = cot_ref.shape[2]
    half = 2 * quarter
    tokens = ib * half
    hj = heads * quarter
    part = rl // 2
    groups = quarter // rl
    score = 1.0 / math.sqrt(width)

    lane_head = lax.broadcasted_iota(jnp.int32, (1, c), 1) // width
    head_masks = [(lane_head == h).astype(FULL) for h in range(heads)]

    def block_diag(v):
        v = v.astype(FULL)
        if part % 16 == 0:
            return jnp.concatenate(
                [(v[g * part : (g + 1) * part] * m).astype(LOW) for g in range(2 * groups) for m in head_masks], axis=0
            )
        rows = jnp.concatenate([v * m for m in head_masks], axis=0).astype(LOW)
        return dot_nn(row_order(quarter, rl, heads).astype(LOW), rows).astype(LOW)

    def pick(t):
        if part % 16:
            order = row_order(quarter, rl, heads).astype(FULL)
            t = lax.dot_general(
                order, t, (((0,), (0,)), ((), ())), precision=lax.Precision.HIGHEST, preferred_element_type=FULL
            )
            size, count = quarter, 1
        else:
            size, count = part, 2 * groups
        parts = []
        for g in range(count):
            base = g * heads * size
            r = t[base + (heads - 1) * size : base + heads * size]
            for h in range(heads - 2, -1, -1):
                r = jnp.where(lane_head == h, t[base + h * size : base + (h + 1) * size], r)
            parts.append(r)
        return jnp.concatenate(parts, axis=0)

    @pl.when(jnp.logical_and(item == 0, blk == 0))
    def _():
        for n, ref in enumerate(grad_refs):
            ref[...] = jnp.zeros_like(ref) if first else rest[n][...]

    @pl.when(blk == 0)
    def _():
        real = lax.broadcasted_iota(jnp.int32, (res, hj), 0) < length
        for jq in range(2):
            b = jnp.concatenate([bias_ref[0, jq, g] for g in range(groups)], axis=1).astype(FULL) * LOG2E
            bias_s[jq] = jnp.where(real, b, -1e9)
        dbias_s[...] = jnp.zeros_like(dbias_s)

    def at(index, size):
        return pl.ds(pl.multiple_of(index * size, size), size)

    g0 = gain_ref[0:1, :]
    g1 = gain_ref[1:2, :]
    g2 = gain_ref[2:3, :]
    g3 = gain_ref[3:4, :]

    def forward(kx):
        cot_s[:, at(core, quarter), :] = cot_ref[0]
        cot_s[:, at(1 - core, quarter), :] = cots_ref[0]
        xq = x_ref[0, :, at(y, half), :].reshape(tokens, c).astype(FULL)
        nq = (normalize(xq)[0] * g0 + g1).astype(LOW)
        nq_s[...] = nq
        qg = dot_nn(nq, wqg_ref[...]).astype(LOW).astype(FULL)
        q_s[...] = (qg[:, :c] * (score * LOG2E)).astype(LOW)
        g_s[...] = jax.nn.sigmoid(qg[:, c:])

        x = x_ref[0, :, :kx, :].reshape(ib * kx, c).astype(FULL)
        n = (normalize(x)[0] * g0 + g1).astype(LOW)
        n_s[: ib * kx] = n
        kv_s[: ib * kx] = dot_nn(n, wkv_ref[...]).astype(LOW)
        ones = jnp.ones((kx, c), LOW)
        units = [(i, jq) for i in range(ib) for jq in range(2)]

        def scores(i, jq):
            row = i * half + jq * quarter
            qbd = block_diag(q_s[row : row + quarter])
            return dot_nt(kv_s[i * kx : (i + 1) * kx, :c], qbd) + bias_s[jq, :kx, :]

        ahead = [scores(*u) for u in units[:depth]]
        for t, (i, jq) in enumerate(units):
            s = ahead.pop(0)
            if t + depth < len(units):
                ahead.append(scores(*units[t + depth]))
            eb = jnp.exp2(s - jnp.max(s, axis=0, keepdims=True)).astype(LOW)
            e_s[i * kx : (i + 1) * kx, jq * hj : (jq + 1) * hj] = eb
            v = kv_s[i * kx : (i + 1) * kx, c:]
            rows = slice(i * half + jq * quarter, i * half + (jq + 1) * quarter)
            o = dot_tn(eb, jnp.concatenate([v, ones], axis=1))
            o_s[rows, :] = pick(o[:, :c])
            r_s[rows, :] = 1.0 / pick(o[:, c:])

    def middle():
        rinv = r_s[...]
        blended = o_s[...] * rinv
        gate = g_s[...]
        gated = (gate * blended).astype(LOW)
        gated_s[...] = gated
        mid = x_ref[0, :, at(y, half), :].reshape(tokens, c).astype(FULL) + dot_nt(gated, wot_ref[...])
        n2, spread = normalize(mid)
        shaped = (n2 * g2 + g3).astype(LOW)
        sh_s[...] = shaped
        hp = dot_nn(shaped, up_ref[...])
        sg = 0.5 * jnp.tanh(0.5 * hp) + 0.5
        silu = hp * sg
        hid = silu.astype(LOW)
        hid_s[...] = hid
        out_s[...] = (mid + dot_nn(hid, down_ref[...])).astype(LOW).reshape(ib, half, c)
        cot = cot_s[...].reshape(tokens, c)
        dh = dot_nt(cot, down_ref[...])
        dpre = (dh * (sg + silu * (1.0 - sg))).astype(LOW)
        dpre_s[...] = dpre
        dsh = dot_nt(dpre, up_ref[...])
        ggain_ref[2:3, :] += jnp.sum(dsh * n2, axis=0, keepdims=True)
        ggain_ref[3:4, :] += jnp.sum(dsh, axis=0, keepdims=True)
        dmid = cot.astype(FULL) + norm_back(dsh * g2, n2, spread)
        dml = dmid.astype(LOW)
        dml_s[...] = dml
        dmid_ref[0] = dml.reshape(ib, half, c)
        dgated = dot_nn(dml, wot_ref[...])
        dblend = dgated * gate
        dqg_s[:, c:] = (dblend * blended * (1.0 - gate)).astype(LOW)
        dos = (dblend * rinv).astype(LOW)
        dos_s[...] = dos
        xn_s[...] = (-dos.astype(FULL) * blended).astype(LOW)
        gdown_ref[...] += dot_tn(cot, hid_s[...])
        gup_ref[...] += dot_tn(sh_s[...], dpre_s[...])
        gout_ref[...] += dot_tn(dml_s[...], gated_s[...])
        res_ref[0] = out_s[:, at(core, quarter), :]
        ress_ref[0] = out_s[:, at(1 - core, quarter), :]

    def backward(kx):
        ones = jnp.ones((kx, c), LOW)
        units = [(i, jq) for i in range(ib) for jq in range(2)]

        def d_scores(i, jq):
            row = i * half + jq * quarter
            dbd = block_diag(dos_s[row : row + quarter])
            xbd = block_diag(xn_s[row : row + quarter])
            v_one = jnp.concatenate([kv_s[i * kx : (i + 1) * kx, c:], ones], axis=1)
            return dot_nt(v_one, jnp.concatenate([dbd, xbd], axis=1)), dbd

        ahead = [d_scores(*u) for u in units[:depth]]
        for t, (i, jq) in enumerate(units):
            dp, dbd = ahead.pop(0)
            if t + depth < len(units):
                ahead.append(d_scores(*units[t + depth]))
            span = slice(i * kx, (i + 1) * kx)
            rows = slice(i * half + jq * quarter, i * half + (jq + 1) * quarter)
            eb = e_s[span, jq * hj : (jq + 1) * hj]
            dl = eb.astype(FULL) * dp
            dbias_s[jq, :kx, :] += dl
            dlb = dl.astype(LOW)
            qbd = block_diag(q_s[rows])
            dqg_s[rows, :c] = (pick(dot_tn(dlb, kv_s[span, :c])) * score).astype(LOW)
            if jq == 0:
                held = (dbd, qbd, dlb)
            else:
                dbd = jnp.concatenate([held[0], dbd], axis=0)
                qbd = jnp.concatenate([held[1], qbd], axis=0)
                dlb = jnp.concatenate([held[2], dlb], axis=1)
                dkv_s[span, c:] = dot_nn(e_s[span, :], dbd).astype(LOW)
                dkv_s[span, :c] = (dot_nn(dlb, qbd) * LN2).astype(LOW)
        dkv = dkv_s[: ib * kx]
        gkv_ref[...] += dot_tn(n_s[: ib * kx], dkv)
        dn_s[:, :kx, :] = dot_nt(dkv, wkv_ref[...]).reshape(ib, kx, c)
        if kx < res:
            dn_s[:, kx:, :] = jnp.zeros((ib, res - kx, c), FULL)
        gqg_ref[...] += dot_tn(nq_s[...], dqg_s[...])
        dn_s[:, at(y, half), :] += dot_nt(dqg_s[...], wqg_ref[...]).reshape(ib, half, c)
        near_ref[0] = dn_s[:, at(y, half), :].astype(LOW)
        far_ref[0] = dn_s[:, at(1 - y, half), :].astype(LOW)

    def step(kx):
        forward(kx)
        middle()
        backward(kx)

    for index, kx in enumerate(variants):
        below = variants[index - 1] if index else 0
        pl.when(jnp.logical_and(length > below, length <= kx))(functools.partial(step, kx))

    @pl.when(blk == pl.num_programs(1) - 1)
    def _():
        lanes = heads * part
        for cc in range(2):
            pieces = []
            for jq in range(2):
                for g in range(groups):
                    for yy in range(2):
                        off = (g * 2 + cc) * lanes
                        t = dbias_s[jq, yy * half : (yy + 1) * half, off : off + lanes]
                        pieces.append(jnp.concatenate([t[:quarter], t[quarter:]], axis=1).astype(LOW))

            @pl.when(core == cc)
            def _():
                for n, t in enumerate(pieces):
                    dbk_ref[n, 0] = t

            @pl.when(core != cc)
            def _():
                for n, t in enumerate(pieces):
                    dbs_ref[n, 0] = t


def main_call(
    start, count, lengths, qidx, pair_rep, cot, cots, bias, weights, grads, result=None, after=(),
    *, ib=8, variants=(128, 256), depth=4,
):
    items, rl, res, c = pair_rep.shape
    quarter = cot.shape[2]
    half = 2 * quarter
    hid = weights[3].shape[1]
    heads = 4
    width = c // heads
    rows = rl // 2
    ib = min(ib, rows)
    tokens = ib * half
    hj = heads * quarter
    steps = rows // ib
    groups = quarter // rl
    n_rows = res // rl
    grad_shapes = [(c, 2 * c), (c, 2 * c), (c, c), (c, hid), (c, hid), (8, c)]

    def whole(shape):
        return pl.BlockSpec(shape, lambda b, i, *_: (0,) * len(shape))

    def own_rows(b, i, ln, q):
        return (start + b, lax.rem(q[0], 2) * steps + i, 0, 0)

    def chunk(size):
        return pl.BlockSpec((1, ib, size, c), lambda b, i, ln, q: (b, i, 0, 0))

    any_spec = pl.BlockSpec(memory_space=pl.ANY)
    cot_spec = pl.BlockSpec((1, ib, quarter, c), own_rows)
    db_spec = pl.BlockSpec((n_rows, 1, quarter, heads * rl), lambda b, i, ln, q: (0, b, 0, 0))
    first = result is None
    extra = () if first else (*grads, result)
    extra_specs = [] if first else [whole(s) for s in grad_shapes] + [any_spec]
    return pl.pallas_call(
        functools.partial(
            main_kernel, start=start, first=first, heads=heads, width=width, rl=rl, variants=variants, depth=depth
        ),
        grid_spec=pltpu.PrefetchScalarGridSpec(
            num_scalar_prefetch=2,
            grid=(count, steps),
            in_specs=[
                pl.BlockSpec((1, ib, res, c), own_rows),
                cot_spec,
                pl.BlockSpec((1, ib, quarter, c), lambda b, i, ln, q: (start + b, i, 0, 0)),
                pl.BlockSpec((1,) + bias.shape[1:], lambda b, i, ln, q: (start + b, 0, 0, 0, 0)),
            ]
            + [whole(w.shape) for w in weights]
            + extra_specs
            + [any_spec] * len(after),
            out_specs=[cot_spec, chunk(quarter), chunk(half), chunk(half), chunk(half), db_spec, db_spec]
            + [whole(s) for s in grad_shapes],
            scratch_shapes=[
                pltpu.VMEM((ib * res, c), LOW),
                pltpu.VMEM((ib * res, 2 * c), LOW),
                pltpu.VMEM((ib * res, 2 * c), LOW),
                pltpu.VMEM((ib * res, 2 * hj), LOW),
                pltpu.VMEM((tokens, c), LOW),
                pltpu.VMEM((tokens, c), LOW),
                pltpu.VMEM((tokens, c), FULL),
                pltpu.VMEM((tokens, c), FULL),
                pltpu.VMEM((tokens, c), FULL),
                pltpu.VMEM((tokens, c), LOW),
                pltpu.VMEM((tokens, c), LOW),
                pltpu.VMEM((tokens, hid), LOW),
                pltpu.VMEM((tokens, hid), LOW),
                pltpu.VMEM((tokens, c), LOW),
                pltpu.VMEM((tokens, c), LOW),
                pltpu.VMEM((tokens, c), LOW),
                pltpu.VMEM((tokens, 2 * c), LOW),
                pltpu.VMEM((2, res, hj), FULL),
                pltpu.VMEM((2, res, hj), FULL),
                pltpu.VMEM((ib, res, c), FULL),
                pltpu.VMEM((ib, half, c), LOW),
                pltpu.VMEM((ib, half, c), LOW),
            ],
        ),
        out_shape=[
            jax.ShapeDtypeStruct((items, rl, quarter, c), LOW),
            jax.ShapeDtypeStruct((count, rows, quarter, c), LOW),
            jax.ShapeDtypeStruct((count, rows, half, c), LOW),
            jax.ShapeDtypeStruct((count, rows, half, c), LOW),
            jax.ShapeDtypeStruct((count, rows, half, c), LOW),
            jax.ShapeDtypeStruct((n_rows, count, quarter, heads * rl), LOW),
            jax.ShapeDtypeStruct((n_rows, count, quarter, heads * rl), LOW),
        ]
        + [jax.ShapeDtypeStruct(s, FULL) for s in grad_shapes],
        input_output_aliases={} if first else {18: 0},
        compiler_params=pltpu.CompilerParams(
            dimension_semantics=("arbitrary", "arbitrary"), vmem_limit_bytes=VMEM_LIMIT
        ),
        cost_estimate=pl.CostEstimate(
            flops=800_000_000 * count * rl, bytes_accessed=300_000 * count * rl, transcendentals=0
        ),
        name="layer",
    )(lengths, qidx, pair_rep, cot, cots, bias, *weights, *extra, *after)


MESH = pl.DeviceIdType.MESH
MOMENTUM = 0.9
AVERAGE = 0.6
RATES = (0.5, 0.3, 3.0, 0.05, 0.03, 0.1)
CHUNKS = (5, 4, 3)


def pad16(n):
    return -(-n // 16) * 16


def greet_all(n_dev, n_heads, me):
    barrier = pltpu.get_barrier_semaphore()

    def signal(s, _):
        d = lax.rem(me + s, n_dev)
        pl.semaphore_signal(barrier, inc=1, device_id=(d // n_heads, lax.rem(d, n_heads)), device_id_type=MESH)
        return 0

    lax.fori_loop(1, n_dev, signal, 0)
    pl.semaphore_wait(barrier, n_dev - 1)


def prep_kernel(
    x_hbm, cot_hbm, proj_ref, bw_ref, out_ref, up_ref, down_ref, gains_ref,
    wkv_ref, wqg_ref, wot_ref, upall_ref, downall_ref, gainall_ref, base_ref, bias_hbm, cots_hbm,
    stage, wbuf, proj_s, up_s, down_s, wot_s, base_s, stack_ref, xbuf, xhat, pbuf, cbuf,
    x_sem, wsend, wrecv, bsend, brecv, self_sem, fsend, frecv, c_sem,
    *, n_rows, n_heads, parts,
):
    items, rl, res, c = x_hbm.shape
    hid = up_ref.shape[1]
    quarter = res // n_heads
    width = out_ref.shape[0]
    n_dev = n_rows * n_heads
    group = n_rows // n_heads
    lanes = n_heads * rl
    r = lax.axis_index("rows")
    q = lax.axis_index("heads")
    me = r * n_heads + q

    def load(b):
        span = pl.ds(pl.multiple_of(q * quarter, quarter), quarter)
        return pltpu.make_async_copy(x_hbm.at[b, :, span, :], xbuf.at[b], x_sem.at[b])

    rows = rl // 2
    other = pl.ds(pl.multiple_of((1 - lax.rem(q, 2)) * rows, rows), rows)
    cot_in = pltpu.make_async_copy(cot_hbm.at[:, other, :, :], cbuf, c_sem.at[0])
    cot_out = pltpu.make_async_remote_copy(
        src_ref=cbuf,
        dst_ref=cots_hbm,
        send_sem=c_sem.at[1],
        recv_sem=c_sem.at[2],
        device_id=(r, q + 1 - 2 * lax.rem(q, 2)),
        device_id_type=MESH,
    )
    for b in range(items):
        load(b).start()
    cot_in.start()

    pr, ur, dr, cr, cd = c // n_rows, c // n_dev, hid // n_dev, c // n_rows, c // n_dev
    o_down = pad16(pr)
    o_up = o_down + pad16(dr)
    o_out = o_up + pad16(ur * (hid // c))
    o_misc = o_out + pad16(cr)
    lane = lax.broadcasted_iota(jnp.int32, (1, c), 1)
    stage[...] = jnp.zeros_like(stage)
    stage[:pr, :] = proj_ref[...]
    stage[o_down : o_down + dr, :] = down_ref[...]
    for g in range(hid // c):
        stage[o_up + g * ur : o_up + (g + 1) * ur, :] = up_ref[:, g * c : (g + 1) * c]
    spot = lax.broadcasted_iota(jnp.int32, (width, c), 1) == q * width + lax.broadcasted_iota(jnp.int32, (width, c), 0)
    stage[o_out : o_out + cr, :] = dot_tn(out_ref[...].astype(LOW), spot.astype(LOW))
    stage[o_misc : o_misc + pr, 0:1] = bw_ref[...]
    stage[o_misc : o_misc + 4, c // 2 : c // 2 + cd] = gains_ref[...]
    wbuf[me] = stage[...].astype(LOW)

    greet_all(n_dev, n_heads, me)

    def weights_to(s):
        d = lax.rem(me + s, n_dev)
        return pltpu.make_async_remote_copy(
            src_ref=wbuf.at[me],
            dst_ref=wbuf.at[me],
            send_sem=wsend.at[s],
            recv_sem=wrecv.at[s],
            device_id=(d // n_heads, lax.rem(d, n_heads)),
            device_id_type=MESH,
        )

    def start_one(s, _):
        weights_to(s).start()
        return 0

    lax.fori_loop(1, n_dev, start_one, 0)

    for b in range(items):
        load(b).wait()
        xhat[b] = normalize(xbuf[b].reshape(rl * quarter, c).astype(FULL))[0]

    cot_in.wait()
    cot_out.start()

    def wait_one(s, _):
        weights_to(s).wait()
        return 0

    lax.fori_loop(1, n_dev, wait_one, 0)

    head_of = lax.rem(lane // (rl // 2), n_heads)
    gain_sum = jnp.zeros((16, c), FULL)
    for rr in range(n_rows):
        wot = jnp.zeros((cr, c), FULL)
        base = jnp.zeros((pr, c), FULL)
        for h in range(n_heads):
            d = rr * n_heads + h
            proj_s[rr * pr : (rr + 1) * pr, h * c : (h + 1) * c] = wbuf[d, :pr].astype(FULL)
            wot = wot + wbuf[d, o_out : o_out + cr].astype(FULL)
            misc = wbuf[d, o_misc : o_misc + 16].astype(FULL)
            base = base + jnp.where(head_of == h, misc[:pr, 0:1], 0.0)
            moved = pltpu.roll(misc, (d * cd + c // 2) % c, 1)
            gain_sum = gain_sum + jnp.where(lane // cd == d, moved, 0.0)
            down_s[d * dr : (d + 1) * dr, :] = wbuf[d, o_down : o_down + dr].astype(FULL)
            for g in range(hid // c):
                rows = slice(o_up + g * ur, o_up + (g + 1) * ur)
                up_s[d * ur : (d + 1) * ur, g * c : (g + 1) * c] = wbuf[d, rows].astype(FULL)
        wot_s[rr * cr : (rr + 1) * cr, :] = wot
        base_s[rr * pr : (rr + 1) * pr, :] = base
    wot_ref[...] = wot_s[...].astype(LOW)
    downall_ref[...] = down_s[...].astype(LOW)
    upall_ref[...] = up_s[...].astype(LOW)
    gainall_ref[...] = gain_sum[:8]
    src = lax.broadcasted_iota(jnp.int32, (n_heads * c, 2 * c), 0)
    dst = lax.broadcasted_iota(jnp.int32, (n_heads * c, 2 * c), 1)
    place = (lax.rem(dst, c) // width) * c + lax.rem(dst, width)
    second = dst // c
    proj_low = proj_s[...].astype(LOW)
    wqg_ref[...] = dot_nn(proj_low, (src == place + second * 3 * width).astype(LOW)).astype(LOW)
    wkv_ref[...] = dot_nn(proj_low, (src == place + width + second * width).astype(LOW)).astype(LOW)
    base = base_s[...]
    row_of = (lane // (rl // 2 * n_heads)) * (rl // 2) + lax.rem(lane, rl // 2)
    base_ref[...] = base[:, :lanes].astype(LOW)
    for jj in range(rl):
        stack_ref[jj * c : (jj + 1) * c, :] = jnp.where(row_of == jj, base, 0.0)[:, :lanes].astype(LOW)

    g0 = gain_sum[0:1]
    g1 = gain_sum[1:2]
    target = r // group
    core = lax.rem(q, 2)
    slot = lax.rem(r, group)
    span = pl.ds(pl.multiple_of(q * quarter, quarter), quarter)
    size = items // parts

    def own_copy(p):
        return pltpu.make_async_copy(
            pbuf.at[pl.ds(p * size, size)], bias_hbm.at[pl.ds(p * size, size), core, slot, span, :], self_sem.at[p]
        )

    def bias_to(p, t, s):
        return pltpu.make_async_remote_copy(
            src_ref=pbuf.at[pl.ds(p * size, size)],
            dst_ref=bias_hbm.at[pl.ds(p * size, size), lax.rem(target, 2), slot, span, :],
            send_sem=bsend.at[p, t],
            recv_sem=brecv.at[p, s],
            device_id=(t, target),
            device_id_type=MESH,
        )

    mine = slot * n_heads + q
    for p in range(parts):

        def piece(b, _):
            n = (xhat[b] * g0 + g1).astype(LOW).reshape(rl, quarter, c)
            wide = jnp.concatenate([n[jj] for jj in range(rl)], axis=1)
            pbuf[b] = dot_nn(wide, stack_ref[...]).astype(LOW)
            return 0

        lax.fori_loop(p * size, (p + 1) * size, piece, 0)

        def send(t, _):
            is_me = jnp.logical_and(t == r, target == q)

            @pl.when(is_me)
            def _():
                own_copy(p).start()

            @pl.when(jnp.logical_not(is_me))
            def _():
                bias_to(p, t, mine).start()

            return 0

        lax.fori_loop(0, n_rows, send, 0)

    def forward(p):
        ref = bias_hbm.at[pl.ds(p * size, size), core]
        return pltpu.make_async_remote_copy(
            src_ref=ref,
            dst_ref=ref,
            send_sem=fsend.at[p],
            recv_sem=frecv.at[p],
            device_id=(r, q + 1 - 2 * core),
            device_id_type=MESH,
        )

    for p in range(parts):

        def finish(t, _):
            is_me = jnp.logical_and(t == r, target == q)

            @pl.when(is_me)
            def _():
                own_copy(p).wait()

            @pl.when(jnp.logical_not(is_me))
            def _():
                bias_to(p, t, mine).wait_send()

            from_me = jnp.logical_and(q * group + t // n_heads == r, lax.rem(t, n_heads) == q)

            @pl.when(jnp.logical_not(from_me))
            def _():
                bias_to(p, t, t).wait_recv()

            return 0

        lax.fori_loop(0, n_rows, finish, 0)
        forward(p).start()

    for p in range(parts):
        forward(p).wait()
    cot_out.wait()


def prep_call(pair_rep, cot, weights, n_rows, n_heads, quarter, parts=3):
    items, rl, res, c = pair_rep.shape
    proj, bw, out, up, down, gains = weights
    hid = up.shape[1]
    n_dev = n_rows * n_heads
    group = n_rows // n_heads
    lanes = n_heads * rl
    width = out.shape[0]
    rows = 2 * pad16(c // n_rows) + pad16(hid // n_dev) + pad16(c // n_dev * (hid // c)) + 16
    vmem = pl.BlockSpec(memory_space=pltpu.VMEM)
    hbm = pl.BlockSpec(memory_space=pl.ANY)
    return pl.pallas_call(
        functools.partial(prep_kernel, n_rows=n_rows, n_heads=n_heads, parts=parts),
        in_specs=[hbm, hbm] + [vmem] * 6,
        out_specs=[vmem] * 7 + [hbm, hbm],
        out_shape=[
            jax.ShapeDtypeStruct((c, 2 * c), LOW),
            jax.ShapeDtypeStruct((c, 2 * c), LOW),
            jax.ShapeDtypeStruct((c, c), LOW),
            jax.ShapeDtypeStruct((c, hid), LOW),
            jax.ShapeDtypeStruct((hid, c), LOW),
            jax.ShapeDtypeStruct((8, c), FULL),
            jax.ShapeDtypeStruct((c, lanes), LOW),
            jax.ShapeDtypeStruct((items, 2, group, res, lanes), LOW),
            jax.ShapeDtypeStruct((items, rl // 2, quarter, c), LOW),
        ],
        scratch_shapes=[
            pltpu.VMEM((rows, c), FULL),
            pltpu.VMEM((n_dev, rows, c), LOW),
            pltpu.VMEM((c, n_heads * c), FULL),
            pltpu.VMEM((c, hid), FULL),
            pltpu.VMEM((hid, c), FULL),
            pltpu.VMEM((c, c), FULL),
            pltpu.VMEM((c, c), FULL),
            pltpu.VMEM((rl * c, lanes), LOW),
            pltpu.VMEM((items, rl, quarter, c), LOW),
            pltpu.VMEM((items, rl * quarter, c), FULL),
            pltpu.VMEM((items, quarter, lanes), LOW),
            pltpu.VMEM((items, rl // 2, quarter, c), LOW),
            pltpu.SemaphoreType.DMA((items,)),
            pltpu.SemaphoreType.DMA((n_dev,)),
            pltpu.SemaphoreType.DMA((n_dev,)),
            pltpu.SemaphoreType.DMA((parts, n_rows)),
            pltpu.SemaphoreType.DMA((parts, n_rows)),
            pltpu.SemaphoreType.DMA((parts,)),
            pltpu.SemaphoreType.DMA((parts,)),
            pltpu.SemaphoreType.DMA((parts,)),
            pltpu.SemaphoreType.DMA((3,)),
        ],
        compiler_params=pltpu.CompilerParams(
            collective_id=0, has_side_effects=True, vmem_limit_bytes=VMEM_LIMIT
        ),
        name="prep",
    )(pair_rep, cot, *weights)


def finish_kernel(
    x_hbm, *refs, n_rows, n_heads, sizes,
):
    n = len(sizes)
    refs = list(refs)
    take = lambda k: [refs.pop(0) for _ in range(k)]
    dmid_hbm, near_hbm, far_hbm, dbk_refs = take(n), take(n), take(n), take(n)
    dbr_refs = take(n - 1)
    (dbs_hbm,) = take(1)
    gqg_ref, gkv_ref, gout_ref, gup_ref, gdown_ref, gtwo_ref, gain_ref, base_ref = take(8)
    pair_hbm, proj_ref, out_ref, up_ref, down_ref, small_ref = take(6)
    xb, mb, nb, fb, ob, sb, dsum, dbuf, xbuf, dtmp, proj_s, down_s, stage, gsrc, gbuf, ggain_s, gbias_s, sbuf = take(18)
    in_sem, far_send, far_recv, pre_sem, xsend, xrecv, dsend, drecv, dself, gsend, grecv, gself, out_sem, osend, orecv, ssend, srecv = refs

    items = sum(sizes)
    starts = [sum(sizes[:i]) for i in range(n)]
    last = n - 1
    n_dev = n_rows * n_heads
    c = gqg_ref.shape[0]
    hid = gup_ref.shape[1]
    width = c // n_heads
    group = n_rows // n_heads
    _, rows, half, _ = xb.shape
    quarter = half // 2
    tokens = rows * half
    lanes = base_ref.shape[1]
    r = lax.axis_index("rows")
    q = lax.axis_index("heads")
    me = r * n_heads + q
    y = q // 2
    core = lax.rem(q, 2)
    sibling = (r, q + 1 - 2 * core)
    across = (r, q + 2 - 4 * y)

    def at(index, size):
        return pl.ds(pl.multiple_of(index * size, size), size)

    loads = []
    for ch in range(n):
        for i in range(sizes[ch]):
            b = starts[ch] + i
            one = [
                pltpu.make_async_copy(x_hbm.at[b, at(core, rows), at(y, half), :], xb.at[b], in_sem.at[0, b]),
                pltpu.make_async_copy(dmid_hbm[ch].at[i], mb.at[b], in_sem.at[1, b]),
                pltpu.make_async_copy(near_hbm[ch].at[i], nb.at[b], in_sem.at[2, b]),
            ]
            if ch != last:
                one.append(pltpu.make_async_copy(far_hbm[ch].at[i], fb.at[b], in_sem.at[3, b]))
            loads += one
    for load in loads:
        load.start()

    greet_all(n_dev, n_heads, me)

    pre = pltpu.make_async_remote_copy(
        src_ref=dbs_hbm,
        dst_ref=dtmp,
        send_sem=pre_sem.at[0],
        recv_sem=pre_sem.at[1],
        device_id=sibling,
        device_id_type=MESH,
    )
    pre.start()

    def far_copy(i):
        return pltpu.make_async_remote_copy(
            src_ref=far_hbm[last].at[i],
            dst_ref=fb.at[starts[last] + i],
            send_sem=far_send.at[i],
            recv_sem=far_recv.at[i],
            device_id=across,
            device_id_type=MESH,
        )

    def db_to(ch, t):
        span = pl.ds(starts[ch], sizes[ch])
        return pltpu.make_async_remote_copy(
            src_ref=dsum.at[t, span],
            dst_ref=dbuf.at[r, span],
            send_sem=dsend.at[ch, t],
            recv_sem=drecv.at[ch, r],
            device_id=(y * 2 * group + t // 2, lax.rem(t, 2) * 2 + core),
            device_id_type=MESH,
        )

    def db_from(ch, t):
        span = pl.ds(starts[ch], sizes[ch])
        return pltpu.make_async_remote_copy(
            src_ref=dsum.at[t, span],
            dst_ref=dbuf.at[t, span],
            send_sem=dsend.at[ch, t],
            recv_sem=drecv.at[ch, t],
            device_id=(t, q),
            device_id_type=MESH,
        )

    def db_own(ch, t):
        span = pl.ds(starts[ch], sizes[ch])
        return pltpu.make_async_copy(dsum.at[t, span], dbuf.at[r, span], dself.at[ch])

    def is_me(t):
        return jnp.logical_and(y * 2 * group + t // 2 == r, lax.rem(t, 2) == y)

    def from_me(t):
        return jnp.logical_and(t == r, r // (2 * group) == y)

    odd = lax.rem(r, 2)
    pairs = n_rows // 2

    def kept(u):
        return (u // 2) * 4 + odd * 2 + lax.rem(u, 2)

    def given(u):
        return (u // 2) * 4 + (1 - odd) * 2 + lax.rem(u, 2)

    def x_to(ch, t):
        span = pl.ds(starts[ch], sizes[ch])
        return pltpu.make_async_remote_copy(
            src_ref=dsum.at[t, span],
            dst_ref=xbuf.at[t, span],
            send_sem=xsend.at[ch, t],
            recv_sem=xrecv.at[ch, t],
            device_id=(r + 1 - 2 * odd, q),
            device_id_type=MESH,
        )

    def x_send(ch):
        def start(u, _):
            x_to(ch, given(u)).start()
            return 0

        lax.fori_loop(0, pairs, start, 0)

    def db_send(ch):
        span = slice(starts[ch], starts[ch] + sizes[ch])

        def start(u, _):
            t = kept(u)
            x_to(ch, given(u)).wait_send()
            x_to(ch, t).wait_recv()
            dsum[t, span] = (dsum[t, span].astype(FULL) + xbuf[t, span].astype(FULL)).astype(LOW)

            @pl.when(is_me(t))
            def _():
                db_own(ch, t).start()

            @pl.when(jnp.logical_not(is_me(t)))
            def _():
                db_to(ch, t).start()

            return 0

        lax.fori_loop(0, pairs, start, 0)

    def db_wait(ch):
        def wait(u, _):
            t = kept(u)
            v = 2 * u + odd

            @pl.when(is_me(t))
            def _():
                db_own(ch, t).wait()

            @pl.when(jnp.logical_not(is_me(t)))
            def _():
                db_to(ch, t).wait_send()

            @pl.when(jnp.logical_not(from_me(v)))
            def _():
                db_from(ch, v).wait_recv()

            return 0

        lax.fori_loop(0, pairs, wait, 0)

    for ch in range(last):
        span = slice(starts[ch], starts[ch] + sizes[ch])
        dsum[:, span] = (dbk_refs[ch][...].astype(FULL) + dbr_refs[ch][...].astype(FULL)).astype(LOW)
        x_send(ch)
    for i in range(sizes[last]):
        far_copy(i).start()
    pre.wait()
    dsum[:, starts[last] :] = (dbk_refs[last][...].astype(FULL) + dtmp[...].astype(FULL)).astype(LOW)
    x_send(last)

    pr, ur, dr, cr = c // n_rows, c // n_dev, hid // n_dev, c // n_rows
    o_down = pad16(pr)
    o_up = o_down + pad16(dr)
    o_out = o_up + pad16(ur * (hid // c))
    wide = n_heads * c
    dst = lax.broadcasted_iota(jnp.int32, (wide, wide), 1)
    kind = lax.rem(dst, c) // width
    spot = jnp.where(kind == 0, 0, jnp.where(kind == 3, 1, kind + 1)) * c + (dst // c) * width + lax.rem(dst, width)
    perm = (lax.broadcasted_iota(jnp.int32, (wide, wide), 0) == spot).astype(LOW)
    mixed = jnp.concatenate([gqg_ref[...].astype(LOW), gkv_ref[...].astype(LOW)], axis=1)
    proj_s[...] = dot_nn(mixed, perm)
    down_s[...] = gdown_ref[...].T
    if pr % 16 or dr % 16 or (ur * (hid // c)) % 16:
        stage[...] = jnp.zeros_like(stage)
    for d in range(n_dev):
        rr, h = d // n_heads, d % n_heads
        stage[d, :pr, :] = proj_s[rr * pr : (rr + 1) * pr, h * c : (h + 1) * c]
        stage[d, o_down : o_down + dr, :] = down_s[d * dr : (d + 1) * dr, :]
        for g in range(hid // c):
            stage[d, o_up + g * ur : o_up + (g + 1) * ur, :] = gup_ref[d * ur : (d + 1) * ur, g * c : (g + 1) * c]
        stage[d, o_out : o_out + cr, :] = gout_ref[rr * cr : (rr + 1) * cr, :]
    gsrc[...] = stage[...].astype(LOW)
    for ch in range(n):
        db_send(ch)

    def to_all(src, dst, sends, recvs, s):
        d = lax.rem(me + s, n_dev)
        return pltpu.make_async_remote_copy(
            src_ref=src.at[d] if src is gsrc else src.at[me],
            dst_ref=dst.at[me],
            send_sem=sends.at[s],
            recv_sem=recvs.at[s],
            device_id=(d // n_heads, lax.rem(d, n_heads)),
            device_id_type=MESH,
        )

    def start_all(*args):
        def start(s, _):
            to_all(*args, s).start()
            return 0

        lax.fori_loop(1, n_dev, start, 0)

    def wait_all(*args):
        def wait(s, _):
            to_all(*args, s).wait()
            return 0

        lax.fori_loop(1, n_dev, wait, 0)

    start_all(gsrc, gbuf, gsend, grecv)
    own = pltpu.make_async_copy(gsrc.at[me], gbuf.at[me], gself.at[0])
    own.start()

    ggain_s[...] = jnp.zeros_like(ggain_s)
    gbias_s[...] = jnp.zeros_like(gbias_s)
    g0 = gain_ref[0:1, :]
    g1 = gain_ref[1:2, :]
    lane = lax.broadcasted_iota(jnp.int32, (1, lanes), 1)
    place = lax.rem(lane, rows) * 2 + lane // (rows * n_heads)

    def pair_local(b):
        return pltpu.make_async_copy(ob.at[b], pair_hbm.at[b, at(core, rows), :, :], out_sem.at[b])

    def pair_remote(b):
        return pltpu.make_async_remote_copy(
            src_ref=sb.at[b],
            dst_ref=pair_hbm.at[b, at(core, rows), :, :],
            send_sem=osend.at[b],
            recv_sem=orecv.at[b],
            device_id=sibling,
            device_id_type=MESH,
        )

    def item(b):
        normal, spread = normalize(xb[b].reshape(tokens, c).astype(FULL))
        normed = (normal * g0 + g1).astype(LOW)
        db = dbuf[odd, b].astype(FULL)
        for t in range(1, pairs):
            db = db + dbuf[2 * t + odd, b].astype(FULL)
        db = db.astype(LOW)
        spread_db = jnp.concatenate([jnp.where(place == t, db, jnp.zeros_like(db)) for t in range(2 * rows)], axis=0)
        gbias_s[...] += dot_tn(normed, spread_db)
        total = nb[b].astype(FULL) + fb[b].astype(FULL)
        dn = total.reshape(tokens, c) + dot_nt(spread_db, base_ref[...])
        ggain_s[0:1, :] += jnp.sum(dn * normal, axis=0, keepdims=True)
        ggain_s[1:2, :] += jnp.sum(dn, axis=0, keepdims=True)
        back = norm_back(dn * g0, normal, spread)
        mb[b] = (mb[b].astype(FULL) + back.reshape(rows, half, c)).astype(LOW)
        ob[b] = mb[b, :, at(core, quarter), :]
        sb[b] = mb[b, :, at(1 - core, quarter), :]
        pair_local(b).start()
        pair_remote(b).start()

    for load in loads:
        load.wait()
    for ch in range(n):
        db_wait(ch)
        if ch == last:
            for i in range(sizes[last]):
                far_copy(i).wait()

        def one(i, _):
            item(starts[ch] + i)
            return 0

        lax.fori_loop(0, sizes[ch], one, 0)

    heads = lax.broadcasted_iota(jnp.int32, (8, lanes), 0) - 2
    sel = (lax.rem(lax.broadcasted_iota(jnp.int32, (8, lanes), 1) // rows, n_heads) == heads).astype(FULL)
    brows = lax.dot_general(
        sel, gbias_s[...], (((1,), (1,)), ((), ())), precision=lax.Precision.HIGHEST, preferred_element_type=FULL
    )
    row = lax.broadcasted_iota(jnp.int32, (8, c), 0)
    two = pltpu.roll(gtwo_ref[...], 4, 0)
    sbuf[me] = jnp.where(row < 2, ggain_s[...], jnp.where(row < 6, brows, two))
    start_all(sbuf, sbuf, ssend, srecv)

    own.wait()
    wait_all(gsrc, gbuf, gsend, grecv)
    total = lax.fori_loop(0, n_dev, lambda d, t: t + gbuf[d].astype(FULL), jnp.zeros(gbuf.shape[1:], FULL))
    proj_ref[...] = total[:pr]
    out_ref[...] = total[o_out : o_out + cr]
    down_ref[...] = total[o_down : o_down + dr]
    for g in range(hid // c):
        up_ref[:, g * c : (g + 1) * c] = total[o_up + g * ur : o_up + (g + 1) * ur]
    wait_all(sbuf, sbuf, ssend, srecv)
    small_ref[...] = lax.fori_loop(0, n_dev, lambda d, t: t + sbuf[d], jnp.zeros(small_ref.shape, FULL))

    def leave(b, _):
        pair_local(b).wait()
        pair_remote(b).wait()
        return 0

    lax.fori_loop(0, items, leave, 0)


def finish_call(pair_rep, dmids, nears, fars, dbks, dbrs, dbs, grads, gains, base, n_rows, n_heads):
    gkv, gqg, gout, gup, gdown, gtwo = grads
    items, rl, res, _ = pair_rep.shape
    c, hid = gup.shape
    n_dev = n_rows * n_heads
    sizes = tuple(t.shape[0] for t in dmids)
    n = len(sizes)
    _, rows, half, _ = dmids[0].shape
    _, count, quarter, lanes = dbs.shape
    pr, ur, dr, cr = c // n_rows, c // n_dev, hid // n_dev, c // n_rows
    grows = 2 * pad16(pr) + pad16(dr) + pad16(ur * (hid // c))
    vmem = pl.BlockSpec(memory_space=pltpu.VMEM)
    hbm = pl.BlockSpec(memory_space=pl.ANY)
    dma = pltpu.SemaphoreType.DMA
    return pl.pallas_call(
        functools.partial(finish_kernel, n_rows=n_rows, n_heads=n_heads, sizes=sizes),
        in_specs=[hbm] * (1 + 3 * n) + [vmem] * (2 * n - 1) + [hbm] + [vmem] * 8,
        out_specs=[hbm] + [vmem] * 5,
        out_shape=[
            jax.ShapeDtypeStruct((items, rl, quarter, c), LOW),
            jax.ShapeDtypeStruct((pr, c), FULL),
            jax.ShapeDtypeStruct((cr, c), FULL),
            jax.ShapeDtypeStruct((ur, hid), FULL),
            jax.ShapeDtypeStruct((dr, c), FULL),
            jax.ShapeDtypeStruct((8, c), FULL),
        ],
        scratch_shapes=[pltpu.VMEM((items, rows, half, c), LOW)] * 4
        + [pltpu.VMEM((items, rows, quarter, c), LOW)] * 2
        + [pltpu.VMEM((n_rows, items, quarter, lanes), LOW)] * 3
        + [
            pltpu.VMEM(dbs.shape, LOW),
            pltpu.VMEM((c, n_heads * c), FULL),
            pltpu.VMEM((hid, c), FULL),
            pltpu.VMEM((n_dev, grows, c), FULL),
            pltpu.VMEM((n_dev, grows, c), LOW),
            pltpu.VMEM((n_dev, grows, c), LOW),
            pltpu.VMEM((8, c), FULL),
            pltpu.VMEM((c, lanes), FULL),
            pltpu.VMEM((n_dev, 8, c), FULL),
            dma((4, items)),
            dma((count,)),
            dma((count,)),
            dma((2,)),
            dma((n, n_rows)),
            dma((n, n_rows)),
            dma((n, n_rows)),
            dma((n, n_rows)),
            dma((n,)),
            dma((n_dev,)),
            dma((n_dev,)),
            dma((1,)),
            dma((items,)),
            dma((items,)),
            dma((items,)),
            dma((n_dev,)),
            dma((n_dev,)),
        ],
        compiler_params=pltpu.CompilerParams(
            collective_id=1, has_side_effects=True, vmem_limit_bytes=VMEM_LIMIT
        ),
        name="finish",
    )(pair_rep, *dmids, *nears, *fars, *dbks, *dbrs, dbs, gqg, gkv, gout, gup, gdown, gtwo, gains, base)


def place_kernel(q_ref, *refs, sizes):
    n = len(sizes)
    parts = refs[1 : 1 + n]
    d_pair, out, out_pair, buf, pair, in_sem, out_sem, pair_in, pair_out = refs[1 + n :]
    rows = buf.shape[1]
    other = pl.ds(pl.multiple_of((1 - lax.rem(q_ref[0], 2)) * rows, rows), rows)
    loads = []
    stores = []
    for b in range(pair.shape[0]):
        loads.append(pltpu.make_async_copy(d_pair.at[b], pair.at[b], pair_in.at[b]))
        stores.append(pltpu.make_async_copy(pair.at[b], out_pair.at[b], pair_out.at[b]))
    for i, size in enumerate(sizes):
        span = pl.ds(sum(sizes[:i]), size)
        loads.append(pltpu.make_async_copy(parts[i], buf.at[span], in_sem.at[i]))
        stores.append(pltpu.make_async_copy(buf.at[span], out.at[span, other, :, :], out_sem.at[i]))
    for load in loads:
        load.start()
    for load, store in zip(loads, stores):
        load.wait()
        store.start()
    for store in stores:
        store.wait()


def place_call(qidx, result, d_pair, results):
    sizes = tuple(t.shape[0] for t in results)
    hbm = pl.BlockSpec(memory_space=pl.ANY)
    dma = pltpu.SemaphoreType.DMA
    return pl.pallas_call(
        functools.partial(place_kernel, sizes=sizes),
        in_specs=[pl.BlockSpec(memory_space=pltpu.SMEM)] + [hbm] * (2 + len(sizes)),
        out_specs=[hbm, hbm],
        out_shape=[jax.ShapeDtypeStruct(result.shape, LOW)] * 2,
        scratch_shapes=[
            pltpu.VMEM((sum(sizes),) + results[0].shape[1:], LOW),
            pltpu.VMEM(d_pair.shape, LOW),
            dma((len(sizes),)),
            dma((len(sizes),)),
            dma((d_pair.shape[0],)),
            dma((d_pair.shape[0],)),
        ],
        input_output_aliases={1: 0},
        compiler_params=pltpu.CompilerParams(vmem_limit_bytes=VMEM_LIMIT),
        name="place",
    )(qidx, result, *results, d_pair)


def update(weight, gradient, moment, average, step_rate, root_pairs):
    moment_next = MOMENTUM * moment + gradient
    weight_next = weight - step_rate / root_pairs * (gradient + MOMENTUM * moment_next)
    return (weight_next, moment_next, AVERAGE * average + (1.0 - AVERAGE) * weight_next)


def shards(
    pair_rep, lengths,
    proj_weight, bias_weight, out_weight, up_weight, down_weight, norm_gains,
    proj_moment, bias_moment, out_moment, up_moment, down_moment, gains_moment,
    proj_average, bias_average, out_average, up_average, down_average, gains_average,
    cotangent,
    *, n_rows, n_heads,
):
    both = ("rows", "heads")
    items, rl, res, c = pair_rep.shape
    quarter = cotangent.shape[2]
    hid = up_weight.shape[1]
    width = out_weight.shape[0]
    n_dev = n_rows * n_heads
    q = lax.axis_index("heads").astype(jnp.int32)
    r = lax.axis_index("rows").astype(jnp.int32)
    qidx = q.reshape(1)
    weights = (proj_weight, bias_weight, out_weight, up_weight, down_weight, norm_gains)
    sibling = [(d, d ^ 1) for d in range(n_dev)]
    across = [(d, d ^ 2) for d in range(n_dev)]
    wkv, wqg, wot, up, down, gains, base, bias, cots = prep_call(
        pair_rep, cotangent, weights, n_rows, n_heads, quarter
    )

    grads = ()
    result = None
    results, dmids, nears, fars, dbks, dbrs = [], [], [], [], [], []
    held = ()
    start = 0
    for n, count in enumerate(CHUNKS):
        outs = main_call(
            start, count, lengths, qidx, pair_rep, cotangent, cots, bias, (wkv, wqg, wot, up, down, gains), grads,
            result, held,
        )
        result, shared, dmid, near, far, dbk, dbs = outs[:7]
        grads = outs[7:]
        results.append(lax.ppermute(shared, both, sibling))
        held = (fars[-1], dbrs[-1]) if n else ()
        if n < len(CHUNKS) - 1:
            far = lax.ppermute(far, both, across)
            dbrs.append(lax.ppermute(dbs, both, sibling))
        dmids.append(dmid)
        nears.append(near)
        fars.append(far)
        dbks.append(dbk)
        start += count

    d_pair, s_proj, s_out, s_up, s_down, small = finish_call(
        pair_rep, dmids, nears, fars, dbks, dbrs, dbs, grads, gains, base, n_rows, n_heads
    )
    result, d_pair = place_call(qidx, result, d_pair, results)
    cd, cr = c // n_dev, c // n_rows
    own = lax.dynamic_slice(small, (0, (r * n_heads + q) * cd), (8, cd))
    s_gains = jnp.concatenate([own[:2], own[6:8]])
    s_bias = lax.dynamic_slice(small, (2 + q, r * cr), (1, cr)).reshape(cr, 1)
    s_out = lax.dynamic_slice(s_out, (0, q * width), (cr, width)).T
    sums = (s_proj, s_bias, s_out, s_up, s_down, s_gains)
    moments = (proj_moment, bias_moment, out_moment, up_moment, down_moment, gains_moment)
    averages = (proj_average, bias_average, out_average, up_average, down_average, gains_average)
    root_pairs = math.sqrt(items * res * res)
    nexts = [
        update(w, g.reshape(w.shape), m, a, rate, root_pairs)
        for w, g, m, a, rate in zip(weights, sums, moments, averages, RATES)
    ]
    return (
        result,
        d_pair,
        *[n[0] for n in nexts],
        *[n[1] for n in nexts],
        *[n[2] for n in nexts],
    )


def solution(mesh):
    weight_specs = (
        P("rows", "heads"),
        P("rows", "heads"),
        P("heads", "rows"),
        P(("rows", "heads"), None),
        P(("rows", "heads"), None),
        P(None, ("rows", "heads")),
    )
    quarter_spec = P(None, "rows", "heads", None)
    in_specs = (P(None, "rows", None, None), P()) + weight_specs * 3 + (quarter_spec,)
    out_specs = (quarter_spec, quarter_spec) + weight_specs * 3
    body = functools.partial(shards, n_rows=mesh.shape["rows"], n_heads=mesh.shape["heads"])
    return jax.shard_map(body, mesh=mesh, in_specs=in_specs, out_specs=out_specs, check_vma=False)
```
